512 devices in a mesh: dp: 8 (over x, core), expert: 64 (over y, z).
Axes of the slice: x: 4, y: 4, z: 16, core: 2. Of those that a mesh axis runs over, the one named last changes fastest.
Arguments:
- tokens: bfloat16 [4096, 2048], P(('dp', 'expert')), may hold values from -6 to 6
- cotangent: bfloat16 [4096, 2048], P(('dp', 'expert')), may hold values from -6 to 6
- expert_ids: int32 [4096, 8], P(('dp', 'expert')), may hold values from 0 to 63, all different within a row; in each aligned block of 8 rows (0 to 7, 8 to 15, ...) at most 2 rows name the same one
- gate_codes: int32 [4096, 8], P(('dp', 'expert')), may hold values from 64 to 1023
- w_gate: bfloat16 [64, 1536, 2048], P('expert', 'dp'), may hold values from -0.125 to 0.125
- w_up: bfloat16 [64, 1536, 2048], P('expert', 'dp'), may hold values from -0.125 to 0.125
- w_down: bfloat16 [64, 1536, 2048], P('expert', 'dp'), may hold values from -0.15625 to 0.15625
Outputs:
- token_grad: bfloat16 [4096, 2048], P(('dp', 'expert'))
- grad_gate: bfloat16 [64, 1536, 2048], P('expert', 'dp')
- grad_up: bfloat16 [64, 1536, 2048], P('expert', 'dp')
- grad_down: bfloat16 [64, 1536, 2048], P('expert', 'dp')
The draws below stay inside these ranges and needn't reach their ends.
Inputs may be any that keep to these rules, and one draw needn't show every extreme that they name: `expert_ids`: each row names 8 different experts; of the 8 rows of one device at most 2 name the same expert, a bound that some block reaches; every expert is named by some row.
All inputs are finite; a program needn't handle non-finite values.
Results may differ from the reference program's by a relative error of at most 0.0065.
Values may be sent and summed in bfloat16 or wider, within the bound.
A program may use at most 64 MiB of HBM per device.

```python
import math
import jax
import jax.numpy as jnp
import numpy as np
from jax import lax

D = 2048
FF = 1536
TOP = 8
TOK_DEV = 8
EXPERTS = 64
CAP = 2
TOKENS = 4096
N_DP = 8


def touch_ends(values, rng, least, high):
    longest = values.shape.index(max(values.shape))
    spots = []
    for shift in (0, 1):
        where = [jax.random.randint(jax.random.fold_in(rng, axis), (), 0, length) for axis, length in enumerate(values.shape)]
        where[longest] = (where[longest] + shift) % values.shape[longest]
        spots.append(tuple(where))
    return values.at[spots[0]].set(least).at[spots[1]].set(high)


def levels(key, shape, shards, low, high):
    loudness, own = 1.0, jax.random.fold_in(key, 6)
    for dim, blocks in shards:
        steps = jnp.exp(jax.random.uniform(jax.random.fold_in(own, dim), (blocks,), jnp.float32, low / len(shards), high / len(shards)))
        loudness = loudness * jnp.repeat(steps, shape[dim] // blocks).reshape([-1 if axis == dim else 1 for axis in range(len(shape))])
    return loudness


def deal_out(stream_key, own, number, rows, number_of, top, bound, lean):
    ranking = jax.random.permutation(stream_key, number_of)
    heavy_load, common = portions_of(number_of, rows * top, bound, lean, True), portions_of(number_of, rows * top, bound, lean, False)
    places = jnp.arange(number_of)

    def named(sizes, rotation):
        used = int((sizes > 0).sum())
        fixed = max(1, used // 4)
        shifted = fixed + (places - fixed + rotation * (used - fixed)) % max(1, number_of - fixed)
        return jnp.zeros((number_of,), jnp.int32).at[ranking[jnp.where(places < fixed, places, shifted)]].set(jnp.asarray(sizes, jnp.int32))

    sizes = jnp.where(number % 4 == 0, named(heavy_load, number // 4), named(common, number - number // 4 - 1))
    mixed = jax.random.permutation(jax.random.fold_in(own, 3), number_of)
    giver, sink = mixed[0:number_of // 2 * 2:2], mixed[1:number_of // 2 * 2:2]
    room = jnp.minimum(sizes[giver] - 1, bound - sizes[sink]) // 2
    room = jnp.where((giver == ranking[0]) | (sink == ranking[0]) | (sizes[sink] == 0), 0, jnp.maximum(room, 0))
    shifted = jax.random.randint(jax.random.fold_in(own, 4), (number_of // 2,), 0, 1 << 20) % (room + 1)
    sizes = sizes.at[giver].add(-shifted).at[sink].add(shifted)
    members = jnp.searchsorted(jnp.cumsum(sizes), jnp.arange(rows * top), side="right").astype(jnp.int32)
    listing = members.reshape(top, rows).T
    listing = listing[jax.random.permutation(jax.random.fold_in(own, 1), rows)]
    rotation = jax.random.randint(jax.random.fold_in(own, 2), (rows, 1), 0, top)
    return jnp.take_along_axis(listing, (jnp.arange(top)[None, :] + rotation) % top, axis=1)


def portions_of(amount, total, most, lean, full):
    portions = [(1 << 20) // math.isqrt(standing ** lean) + 1 for standing in range(1, amount + 1)]
    largest = most if full else min(most, max(-(-total // amount), total * portions[0] // sum(portions)))
    least = 1 if total - largest >= amount - 1 else 0
    holding, surplus = [largest] + [least] * (amount - 1), total - largest - least * (amount - 1)
    while surplus > 0:
        free = [i for i in range(1, amount) if holding[i] < largest] or [i for i in range(1, amount) if holding[i] < most]
        whole, remaining = sum([portions[i] for i in free]), surplus
        for i in free:
            more = min(most - holding[i], max(1, remaining * portions[i] // whole), surplus)
            holding[i] = holding[i] + more
            surplus = surplus - more
    return np.array(holding)


def scatter_about(key, shape, width, reach, shards=(), kind=jnp.bfloat16):
    array = jax.random.normal(key, shape, jnp.float32) * width
    if len(shards) > 0:
        array = levels(key, shape, shards, -0.22, 0.18) * array
    return jnp.clip(array, min=-reach, max=reach).astype(kind)


def setup_inputs(seed: int = 0) -> dict:
    arg_keys = jax.random.split(jax.random.key(seed), 8)
    tokens = scatter_about(arg_keys[0], (TOKENS, D), 1.0, 6.0, ((0, 512),))
    cotangent = scatter_about(arg_keys[1], (TOKENS, D), 1.0, 6.0, ((0, 512),))
    expert_ids_keys = jax.random.split(jax.random.fold_in(arg_keys[2], 1), TOKENS // TOK_DEV)
    expert_ids_turns = jax.random.permutation(jax.random.fold_in(arg_keys[2], 3), TOKENS // TOK_DEV)
    expert_ids = jax.vmap(lambda own, number: deal_out(jax.random.fold_in(arg_keys[2], 2), own, number, TOK_DEV, EXPERTS, TOP, CAP, 2))(expert_ids_keys, expert_ids_turns).reshape((TOKENS, TOP))
    gate_codes = touch_ends(jax.random.randint(arg_keys[3], (TOKENS, TOP), 64, 1024), jax.random.fold_in(arg_keys[3], 1), 64, 1023).astype(jnp.int32)
    w_gate = scatter_about(arg_keys[4], (EXPERTS, FF, D), D ** -0.5, 0.125, ((0, 64), (1, 8)))
    w_up = scatter_about(arg_keys[5], (EXPERTS, FF, D), D ** -0.5, 0.125, ((0, 64), (1, 8)))
    w_down = scatter_about(arg_keys[6], (EXPERTS, FF, D), FF ** -0.5, 0.15625, ((0, 64), (1, 8)))
    return {"tokens": tokens, "cotangent": cotangent, "expert_ids": expert_ids, "gate_codes": gate_codes, "w_gate": w_gate, "w_up": w_up, "w_down": w_down}


gate_unit = 1.0 / 1024.0


def expert_terms(inputs, cot_rows, weight_gate, weight_up, weight_down):
    pre_gate = jnp.dot(inputs, weight_gate.T, preferred_element_type=jnp.float32)
    pre_up = jnp.dot(inputs, weight_up.T, preferred_element_type=jnp.float32)
    sigmoid_gate = jax.nn.sigmoid(pre_gate)
    active = pre_gate * sigmoid_gate
    hidden = (active * pre_up).astype(jnp.bfloat16)
    d_hidden = jnp.dot(cot_rows, weight_down.T, preferred_element_type=jnp.float32)
    d_up = (d_hidden * active).astype(jnp.bfloat16)
    d_gate = (d_hidden * pre_up * sigmoid_gate * (1.0 + pre_gate * (1.0 - sigmoid_gate))).astype(jnp.bfloat16)
    return hidden, d_gate, d_up


def reference(tokens, cotangent, expert_ids, gate_codes, w_gate, w_up, w_down):
    block_rows = 256
    slice_width = FF // N_DP
    flat_ids = expert_ids.reshape(-1).astype(jnp.int32)
    order = jnp.argsort(flat_ids, stable=True).astype(jnp.int32)
    owners = (order // TOP).astype(jnp.int32)
    scales = gate_codes.reshape(-1)[order].astype(jnp.float32) * gate_unit
    tallies = jnp.sum((flat_ids[:, None] == jnp.arange(EXPERTS, dtype=jnp.int32)[None, :]).astype(jnp.int32), axis=0)
    starts = (jnp.cumsum(tallies) - tallies).astype(jnp.int32)
    zero_grads = jnp.zeros((FF, D), jnp.float32)

    def per_expert(token_acc, expert):
        weight_gate = w_gate[expert]
        weight_up = w_up[expert]
        weight_down = w_down[expert]
        slices_gate = weight_gate.astype(jnp.float32).reshape(N_DP, slice_width, D)
        slices_up = weight_up.astype(jnp.float32).reshape(N_DP, slice_width, D)
        first = starts[expert]
        total = tallies[expert]

        def one_block(block_index, state):
            token_acc, sum_gate, sum_up, sum_down = state
            positions = first + block_index * block_rows + jnp.arange(block_rows, dtype=jnp.int32)
            inside = positions < first + total
            clipped = jnp.where(inside, positions, 0).astype(jnp.int32)
            owner_rows = owners[clipped]
            inputs = jnp.where(inside[:, None], tokens[owner_rows], jnp.zeros((), jnp.bfloat16))
            factors = jnp.where(inside, scales[clipped], jnp.zeros((), jnp.float32))
            cot_rows = (factors[:, None] * cotangent[owner_rows].astype(jnp.float32)).astype(jnp.bfloat16)
            hidden, d_gate, d_up = expert_terms(inputs, cot_rows, weight_gate, weight_up, weight_down)
            pieces = jnp.einsum("rpf,pfd->rpd", d_gate.astype(jnp.float32).reshape(block_rows, N_DP, slice_width), slices_gate)
            pieces = pieces + jnp.einsum("rpf,pfd->rpd", d_up.astype(jnp.float32).reshape(block_rows, N_DP, slice_width), slices_up)
            pieces = lax.optimization_barrier(pieces.astype(jnp.bfloat16)).astype(jnp.float32)
            added = jnp.where(inside[:, None], jnp.sum(pieces, axis=1), jnp.zeros((), jnp.float32))
            token_acc = token_acc.at[owner_rows].add(added)
            sum_gate = sum_gate + jnp.dot(d_gate.T, inputs, preferred_element_type=jnp.float32)
            sum_up = sum_up + jnp.dot(d_up.T, inputs, preferred_element_type=jnp.float32)
            sum_down = sum_down + jnp.dot(hidden.T, cot_rows, preferred_element_type=jnp.float32)
            return token_acc, sum_gate, sum_up, sum_down

        blocks = (total + block_rows - 1) // block_rows
        token_acc, sum_gate, sum_up, sum_down = lax.fori_loop(0, blocks, one_block, (token_acc, zero_grads, zero_grads, zero_grads))
        return token_acc, (sum_gate.astype(jnp.bfloat16), sum_up.astype(jnp.bfloat16), sum_down.astype(jnp.bfloat16))

    token_acc, grads = lax.scan(per_expert, jnp.zeros(tokens.shape, jnp.float32), jnp.arange(EXPERTS, dtype=jnp.int32))
    return token_acc.astype(jnp.bfloat16), grads[0], grads[1], grads[2]
```

```python
import jax
import jax.numpy as jnp
from jax import lax
from jax.sharding import PartitionSpec as P

gate_unit = 1.0 / 1024.0
slots = 2


def slot_tables(route_ids, route_codes, experts):
    rows_here, top_here = route_ids.shape
    flat_ids = route_ids.reshape(-1)
    hits = (flat_ids[:, None] == jnp.arange(experts, dtype=jnp.int32)[None, :]).astype(jnp.int32)
    ranks = jnp.sum((jnp.cumsum(hits, axis=0) - 1) * hits, axis=1)
    by_slot = (ranks[:, None] == jnp.arange(slots, dtype=jnp.int32)[None, :]).astype(jnp.float32)
    hit_table = hits.astype(jnp.float32).reshape(rows_here, top_here, experts)
    slot_table = by_slot.reshape(rows_here, top_here, slots)
    select = jnp.einsum("gie,gis->esg", hit_table, slot_table)
    factors = route_codes.astype(jnp.float32) * gate_unit
    weights = jnp.einsum(
        "gie,gis,gi->es", hit_table, slot_table, factors, precision=lax.Precision.HIGHEST
    )
    return (select.astype(jnp.bfloat16), weights)


def fill_slots(select, weights, rows_in, rows_cot):
    in_slots = jnp.einsum(
        "esg,gd->esd", select, rows_in, preferred_element_type=jnp.float32
    ).astype(jnp.bfloat16)
    cot_slots = jnp.einsum("esg,gd->esd", select, rows_cot, preferred_element_type=jnp.float32)
    cot_slots = (weights[:, :, None] * cot_slots).astype(jnp.bfloat16)
    return (in_slots, cot_slots)


def expert_pass(inputs, cot_rows, weight_gate, weight_up, weight_down):
    feature_contract = (((1,), (1,)), ((), ()))
    row_contract = (((0,), (0,)), ((), ()))
    pre_gate = lax.dot_general(
        inputs, weight_gate, feature_contract, preferred_element_type=jnp.float32
    )
    pre_up = lax.dot_general(
        inputs, weight_up, feature_contract, preferred_element_type=jnp.float32
    )
    sigmoid_gate = jax.nn.sigmoid(pre_gate)
    active = pre_gate * sigmoid_gate
    hidden = (active * pre_up).astype(jnp.bfloat16)
    d_hidden = lax.dot_general(
        cot_rows, weight_down, feature_contract, preferred_element_type=jnp.float32
    )
    d_up = (d_hidden * active).astype(jnp.bfloat16)
    d_gate = (d_hidden * pre_up * sigmoid_gate * (1.0 + pre_gate * (1.0 - sigmoid_gate))).astype(
        jnp.bfloat16
    )
    grad_down = lax.dot_general(hidden, cot_rows, row_contract, preferred_element_type=jnp.float32)
    grad_gate = lax.dot_general(d_gate, inputs, row_contract, preferred_element_type=jnp.float32)
    grad_up = lax.dot_general(d_up, inputs, row_contract, preferred_element_type=jnp.float32)
    partial_value = jnp.dot(d_gate, weight_gate, preferred_element_type=jnp.float32)
    partial_value = partial_value + jnp.dot(d_up, weight_up, preferred_element_type=jnp.float32)
    return (partial_value, grad_gate, grad_up, grad_down)


def body(tokens, cotangent, expert_ids, gate_codes, w_gate, w_up, w_down):
    width = tokens.shape[1]
    experts = lax.axis_size("expert")
    select, weights = slot_tables(expert_ids, gate_codes, experts)
    in_slots, cot_slots = fill_slots(select, weights, tokens, cotangent)
    got_in = lax.all_to_all(in_slots, "expert", split_axis=0, concat_axis=0, tiled=True)
    got_cot = lax.all_to_all(cot_slots, "expert", split_axis=0, concat_axis=0, tiled=True)
    all_in = lax.all_gather(got_in.reshape(-1, width), "dp", axis=0, tiled=True)
    all_cot = lax.all_gather(got_cot.reshape(-1, width), "dp", axis=0, tiled=True)
    partial_value, grad_gate, grad_up, grad_down = expert_pass(
        all_in, all_cot, w_gate[0], w_up[0], w_down[0]
    )
    summed = lax.psum_scatter(partial_value, "dp", scatter_dimension=0, tiled=True)
    returned = lax.all_to_all(
        summed.astype(jnp.bfloat16).reshape(experts, slots, width),
        "expert",
        split_axis=0,
        concat_axis=0,
        tiled=True,
    )
    token_grad = jnp.einsum("esg,esd->gd", select, returned, preferred_element_type=jnp.float32)
    return (
        token_grad.astype(jnp.bfloat16),
        grad_gate[None].astype(jnp.bfloat16),
        grad_up[None].astype(jnp.bfloat16),
        grad_down[None].astype(jnp.bfloat16),
    )


def solution(mesh):
    placed = (
        P(("dp", "expert"), None),
        P(("dp", "expert"), None),
        P(("dp", "expert"), None),
        P(("dp", "expert"), None),
        P("expert", "dp", None),
        P("expert", "dp", None),
        P("expert", "dp", None),
    )
    return jax.shard_map(
        body,
        mesh=mesh,
        in_specs=placed,
        out_specs=(
            P(("dp", "expert"), None),
            P("expert", "dp", None),
            P("expert", "dp", None),
            P("expert", "dp", None),
        ),
        check_vma=False,
    )
```

```python
import functools

import jax
import jax.numpy as jnp
from jax import lax
from jax.experimental import pallas as pl
from jax.experimental.pallas import tpu as pltpu
from jax.sharding import PartitionSpec as P

MESH = pl.DeviceIdType.MESH
f32 = jnp.float32
bf16 = jnp.bfloat16

D = 2048
H = 192
NX, NY, NZ = 4, 4, 16
META = 128
HALF = D // 2
PIECE = 16
PLANE = NY * PIECE
COPIES = 192

OFFSETS = (0, -1, 1, -2, 2, -3, 3, -4, 4, -5, 5, -6, 6, -7, 7, -8)
POS = {offset: place for place, offset in enumerate(OFFSETS)}


def dot_nt(a, b):
    return lax.dot_general(a, b, (((1,), (1,)), ((), ())), preferred_element_type=f32)


def dot(a, b):
    return jnp.dot(a, b, preferred_element_type=f32)


def kernel(
    tok_ref, cot_ref, ids_ref, codes_ref, wg_ref, wu_ref, wd_ref,
    tg_ref, gg_ref, gu_ref, gd_ref,
    gz, sel, unsel, xc, h_t, dg_t, du_t, p_own, p_sib, p_got,
    xs_o, xs_l, xs_r, xr_o, xr_l, xr_r, ys, yr, zp, zs_m, zs_p, zr_m, zr_p,
    send_sem, recv_sem,
):
    me_dp = lax.axis_index("dp")
    me_e = lax.axis_index("expert")
    x, core = me_dp // 2, me_dp % 2
    y, z = me_e // NZ, me_e % NZ

    def at(dx=0, dy=0, dz=0, flip=False):
        other = (1 - core) if flip else core
        return (
            ((x + dx + NX) % NX) * 2 + other,
            ((y + dy + NY) % NY) * NZ + (z + dz + NZ) % NZ,
        )

    x_up, x_dn = at(dx=1), at(dx=-1)
    z_up, z_dn = at(dz=1), at(dz=-1)
    sibling = at(flip=True)
    y_peer = {1: at(dy=1), 2: at(dy=-1), 3: at(dy=2)}
    y_back = {1: at(dy=-1), 2: at(dy=1), 3: at(dy=2)}

    counter = [0]
    started = []

    def copy(src, dst, device):
        number = counter[0]
        counter[0] += 1
        made = pltpu.make_async_remote_copy(
            src_ref=src, dst_ref=dst, send_sem=send_sem.at[number],
            recv_sem=recv_sem.at[number], device_id=device, device_id_type=MESH,
        )
        started.append(made)
        made.start()
        return made

    barrier = pltpu.get_barrier_semaphore()
    partners = (z_up, z_dn, at(dy=1), at(dy=-1), at(dy=2), x_up, x_dn, sibling)
    for partner in partners:
        pl.semaphore_signal(barrier, inc=1, device_id=partner, device_id_type=MESH)

    rows = jnp.concatenate([tok_ref[...].astype(f32), cot_ref[...].astype(f32)], axis=0)
    gz[0, :, 0:D] = rows.astype(bf16)
    codes = codes_ref[...]
    parts = (ids_ref[...], codes // 8, codes % 8)
    spread_row = lax.broadcasted_iota(jnp.int32, (8, META), 0)
    spread_col = lax.broadcasted_iota(jnp.int32, (8, META), 1)
    meta = jnp.zeros((8, META), f32)
    for number, part in enumerate(parts):
        spread = (spread_col == spread_row + 8 * number).astype(f32)
        meta = meta + dot(part.astype(f32).astype(bf16), spread.astype(bf16))
    gz[0, :, D:D + META] = jnp.concatenate([meta, meta], axis=0).astype(bf16)

    pl.semaphore_wait(barrier, len(partners))

    cuts = ((0, HALF), (HALF, D + META - HALF))

    def z_send(place, to_place, device):
        return [
            copy(
                gz.at[place, :, pl.ds(first, size)],
                gz.at[to_place, :, pl.ds(first, size)],
                device,
            )
            for first, size in cuts
        ]

    up = z_send(POS[0], POS[-1], z_up)
    down = z_send(POS[0], POS[1], z_dn)

    def z_step(k, up, down):
        next_up, next_down = [], []
        for cut, (first, size) in enumerate(cuts):
            up[cut].wait_recv()
            if k < 8:
                next_up.append(copy(
                    gz.at[POS[-k], :, pl.ds(first, size)],
                    gz.at[POS[-k - 1], :, pl.ds(first, size)], z_up))
            if k <= 7:
                down[cut].wait_recv()
            if k < 7:
                next_down.append(copy(
                    gz.at[POS[k], :, pl.ds(first, size)],
                    gz.at[POS[k + 1], :, pl.ds(first, size)], z_dn))
        return next_up, next_down

    lane = lax.broadcasted_iota(jnp.int32, (128, 128), 1)
    row = lax.broadcasted_iota(jnp.int32, (128, 128), 0)
    lane_kind, lane_dy, lane_slot = lane // 64, (lane % 64) // 16, lane % 16
    step_y = jnp.where(lane_dy == 1, 1, jnp.where(lane_dy == 2, NY - 1, jnp.where(lane_dy == 3, 2, 0)))
    lane_expert = (((y + step_y) % NY) * NZ + z).astype(f32)
    fits = (lane_kind == (row % 16) // 8) & (row // 16 == lane_slot // 2)
    earlier = ((row // 8 == lane // 8) & (lane < row)).astype(f32).astype(bf16)
    lane_rank = (lane_slot % 2).astype(f32)

    def base(c, q):
        return (c * 8 + q) * PLANE

    def select(c):
        block = gz[8 * c:8 * c + 8]
        table = block[:, :, D:D + META].reshape(128, META).astype(f32)
        hit = jnp.zeros((128, 128), f32)
        high = jnp.zeros((128, 128), f32)
        low = jnp.zeros((128, 128), f32)
        for i in range(8):
            same = table[:, i:i + 1] == lane_expert
            hit = hit + jnp.where(same, 1.0, 0.0)
            high = high + jnp.where(same, table[:, 8 + i:9 + i], 0.0)
            low = low + jnp.where(same, table[:, 16 + i:17 + i], 0.0)
        rank = dot(earlier, hit.astype(bf16))
        mine = jnp.where(fits & (rank == lane_rank), hit, 0.0)
        unsel[c] = mine.astype(bf16)
        is_cot = lane_kind == 1
        first = (mine * jnp.where(is_cot, high * (1.0 / 128.0), 1.0)).T.astype(bf16)
        second = (mine * jnp.where(is_cot, low * (1.0 / 1024.0), 0.0)).T.astype(bf16)
        for j in range(4):
            cols = pl.ds(512 * j, 512)
            data = gz[8 * c:8 * c + 8, :, cols].reshape(128, 512)
            got = (dot(first, data) + dot(second, data)).astype(bf16)
            for kind in range(2):
                to = pl.ds(kind * D + 512 * j, 512)
                xc[pl.ds(base(c, 0), PIECE), to] = got[64 * kind:64 * kind + 16]
                sel[c, :, :, to] = got[64 * kind + 16:64 * kind + 64].reshape(3, 16, 512)

    def y_send(c):
        return {
            p: copy(sel.at[c, p - 1], xc.at[pl.ds(base(c, 0) + p * PIECE, PIECE), :], y_peer[p])
            for p in (1, 2, 3)
        }

    def piece(c, q, p):
        return xc.at[pl.ds(base(c, q) + p * PIECE, PIECE), :]

    def half_piece(c, q, p, kind):
        return xc.at[pl.ds(base(c, q) + p * PIECE, PIECE), pl.ds(kind * D, D)]

    from_dn, from_up, far_in, far_cot, sib = {}, {}, {}, {}, {}

    def x_first(c, p):
        from_dn[c, p] = copy(piece(c, 0, p), piece(c, 1, p), x_up)
        from_up[c, p] = copy(piece(c, 0, p), piece(c, 2, p), x_dn)
        sib[c, 0, p] = copy(piece(c, 0, p), piece(c, 4, p), sibling)

    def x_forward(c, p):
        from_dn[c, p].wait_recv()
        far_in[c, p] = copy(half_piece(c, 1, p, 0), half_piece(c, 3, p, 0), x_up)
        sib[c, 1, p] = copy(piece(c, 1, p), piece(c, 5, p), sibling)
        from_up[c, p].wait_recv()
        far_cot[c, p] = copy(half_piece(c, 2, p, 1), half_piece(c, 3, p, 1), x_dn)
        sib[c, 2, p] = copy(piece(c, 2, p), piece(c, 6, p), sibling)

    def x_last(c, p):
        far_in[c, p].wait_recv()
        far_cot[c, p].wait_recv()
        sib[c, 3, p] = copy(piece(c, 3, p), piece(c, 7, p), sibling)

    def forward(c, half):
        if half == 1:
            for q in range(4):
                for p in range(4):
                    sib[c, q, p].wait_recv()
        first = base(c, 4 * half)
        rows_here = pl.ds(first, 256)
        pre_gate = dot_nt(xc[rows_here, 0:D], wg_ref[0])
        pre_up = dot_nt(xc[rows_here, 0:D], wu_ref[0])
        d_hidden = dot_nt(xc[rows_here, D:2 * D], wd_ref[0])
        sig = jax.nn.sigmoid(pre_gate)
        active = pre_gate * sig
        hidden = active * pre_up
        d_up = d_hidden * active
        d_gate = d_hidden * pre_up * sig * (1.0 + pre_gate * (1.0 - sig))
        h_t[:, rows_here] = hidden.T.astype(bf16)
        du_t[:, rows_here] = d_up.T.astype(bf16)
        dg_t[:, rows_here] = d_gate.T.astype(bf16)
        d_up, d_gate = d_up.astype(bf16), d_gate.astype(bf16)
        into = p_sib if half else p_own
        for j in range(4):
            cols = pl.ds(512 * j, 512)
            part = dot(d_gate, wg_ref[0, :, cols]) + dot(d_up, wu_ref[0, :, cols])
            into[c, :, cols] = part.astype(bf16)

    def core_send(c):
        return {
            q: copy(p_sib.at[c, pl.ds(q * PLANE, PLANE)], p_got.at[c, pl.ds(q * PLANE, PLANE)], sibling)
            for q in (3, 2, 1, 0)
        }

    def pair(c, q, cols):
        here = pl.ds(q * PLANE, PLANE)
        return p_own[c, here, cols].astype(f32) + p_got[c, here, cols].astype(f32)

    left, right, both = pl.ds(0, HALF), pl.ds(HALF, HALF), pl.ds(0, D)

    def x_return_first(c, core_copies):
        core_copies[3].wait_recv()
        xs_o[c] = pair(c, 3, both).astype(bf16)
        relay_r = copy(xs_o.at[c, :, left], xr_o.at[c, :, left], x_up)
        relay_l = copy(xs_o.at[c, :, right], xr_o.at[c, :, right], x_dn)
        core_copies[2].wait_recv()
        xs_r[c, :, right] = pair(c, 2, right).astype(bf16)
        r_plain = copy(xs_r.at[c, :, right], xr_l.at[c, :, right], x_up)
        core_copies[1].wait_recv()
        xs_l[c, :, left] = pair(c, 1, left).astype(bf16)
        l_plain = copy(xs_l.at[c, :, left], xr_r.at[c, :, left], x_dn)
        return relay_r, relay_l, r_plain, l_plain

    def x_return_second(c, relay_r, relay_l, r_plain, l_plain):
        relay_r.wait_recv()
        xs_r[c, :, left] = (pair(c, 2, left) + xr_o[c, :, left].astype(f32)).astype(bf16)
        r_sum = copy(xs_r.at[c, :, left], xr_l.at[c, :, left], x_up)
        relay_l.wait_recv()
        xs_l[c, :, right] = (pair(c, 1, right) + xr_o[c, :, right].astype(f32)).astype(bf16)
        l_sum = copy(xs_l.at[c, :, right], xr_r.at[c, :, right], x_dn)
        return r_plain, l_plain, r_sum, l_sum

    def y_return(c, core_copies, arriving):
        core_copies[0].wait_recv()
        for one in arriving:
            one.wait_recv()
        sends = {}
        for side, cols in enumerate((left, right)):
            total = pair(c, 0, cols) + xr_l[c, :, cols].astype(f32) + xr_r[c, :, cols].astype(f32)
            total = total.astype(bf16)
            yr[c, side, 0] = total[0:PIECE]
            ys[c, side] = total[PIECE:].reshape(3, PIECE, HALF)
        for p in (3, 1, 2):
            sends[p] = copy(ys.at[c, :, p - 1], yr.at[c, :, p], y_back[p])
        return sends

    def unselect(c, y_copies):
        for p in (1, 2, 3):
            y_copies[p].wait_recv()
        part = dot(unsel[c], yr[c].reshape(128, HALF))
        zp[8 * c:8 * c + 8] = part.reshape(8, 16, HALF)

    def grad_tile(kind, j):
        out, lhs, shift = ((gg_ref, dg_t, 0), (gu_ref, du_t, 0), (gd_ref, h_t, D))[kind]
        data = xc[:, pl.ds(shift + 512 * j, 512)]
        out[0, :, pl.ds(512 * j, 512)] = dot(lhs[...], data).astype(bf16)

    tiles = [(kind, j) for kind in range(3) for j in range(4)]

    def some_grads(count):
        for _ in range(min(count, len(tiles))):
            grad_tile(*tiles.pop(0))

    for k in range(1, 5):
        up, down = z_step(k, up, down)
    select(0)
    y0 = y_send(0)
    x_first(0, 0)
    up, down = z_step(5, up, down)
    y0[1].wait_recv()
    x_first(0, 1)
    y0[2].wait_recv()
    x_first(0, 2)
    up, down = z_step(6, up, down)
    y0[3].wait_recv()
    x_first(0, 3)
    x_forward(0, 0)
    up, down = z_step(7, up, down)
    x_forward(0, 1)
    up, down = z_step(8, up, down)
    select(1)
    y1 = y_send(1)
    x_first(1, 0)
    x_last(0, 0)
    x_forward(0, 2)
    y1[1].wait_recv()
    x_first(1, 1)
    y1[2].wait_recv()
    x_first(1, 2)
    y1[3].wait_recv()
    x_first(1, 3)
    x_last(0, 1)
    x_forward(0, 3)
    x_last(0, 2)
    x_forward(1, 0)
    x_last(0, 3)
    forward(0, 0)
    x_forward(1, 1)
    forward(0, 1)
    x_forward(1, 2)
    core0 = core_send(0)
    x_last(1, 0)
    x_forward(1, 3)
    x_last(1, 1)
    x0 = x_return_first(0, core0)
    x_last(1, 2)
    x_last(1, 3)
    forward(1, 0)
    x0 = x_return_second(0, *x0)
    forward(1, 1)
    core1 = core_send(1)
    back0 = y_return(0, core0, x0)
    x1 = x_return_first(1, core1)
    some_grads(2)
    x1 = x_return_second(1, *x1)
    unselect(0, back0)
    some_grads(2)
    back1 = y_return(1, core1, x1)
    some_grads(2)
    unselect(1, back1)

    got_m, got_p = None, None
    for j in range(8):
        block = zp[POS[-(8 - j)]]
        if got_m is not None:
            got_m.wait_recv()
            block = block + zr_m[j - 1]
        zs_m[j] = block
        got_m = copy(zs_m.at[j], zr_m.at[j], z_dn)
        if j < 7:
            block = zp[POS[7 - j]]
            if got_p is not None:
                got_p.wait_recv()
                block = block + zr_p[j - 1]
            zs_p[j] = block
            got_p = copy(zs_p.at[j], zr_p.at[j], z_up)
        some_grads(1)
    some_grads(len(tiles))
    got_p.wait_recv()
    got_m.wait_recv()
    total = zp[0] + zr_m[7] + zr_p[6]
    tg_ref[:, 0:HALF] = total[0:8].astype(bf16)
    tg_ref[:, HALF:D] = total[8:16].astype(bf16)

    for made in started:
        made.wait_send()


def body(tokens, cotangent, expert_ids, gate_codes, w_gate, w_up, w_down):
    vmem = pl.BlockSpec(memory_space=pltpu.VMEM)
    return pl.pallas_call(
        kernel,
        out_shape=(
            jax.ShapeDtypeStruct((8, D), bf16),
            jax.ShapeDtypeStruct((1, H, D), bf16),
            jax.ShapeDtypeStruct((1, H, D), bf16),
            jax.ShapeDtypeStruct((1, H, D), bf16),
        ),
        in_specs=[vmem] * 7,
        out_specs=(vmem,) * 4,
        scratch_shapes=[
            pltpu.VMEM((NZ, 16, D + META), bf16),
            pltpu.VMEM((2, 3, PIECE, 2 * D), bf16),
            pltpu.VMEM((2, 128, 128), bf16),
            pltpu.VMEM((1024, 2 * D), bf16),
            pltpu.VMEM((H, 1024), bf16),
            pltpu.VMEM((H, 1024), bf16),
            pltpu.VMEM((H, 1024), bf16),
            pltpu.VMEM((2, 256, D), bf16),
            pltpu.VMEM((2, 256, D), bf16),
            pltpu.VMEM((2, 256, D), bf16),
        ]
        + [pltpu.VMEM((2, PLANE, D), bf16)] * 6
        + [
            pltpu.VMEM((2, 2, 3, PIECE, HALF), bf16),
            pltpu.VMEM((2, 2, 4, PIECE, HALF), bf16),
            pltpu.VMEM((NZ, 16, HALF), f32),
            pltpu.VMEM((8, 16, HALF), f32),
            pltpu.VMEM((7, 16, HALF), f32),
            pltpu.VMEM((8, 16, HALF), f32),
            pltpu.VMEM((7, 16, HALF), f32),
            pltpu.SemaphoreType.DMA((COPIES,)),
            pltpu.SemaphoreType.DMA((COPIES,)),
        ],
        compiler_params=pltpu.CompilerParams(
            collective_id=0, has_side_effects=True, vmem_limit_bytes=52 * 1024 * 1024
        ),
        name="expert_layer_backward",
    )(tokens, cotangent, expert_ids, gate_codes, w_gate, w_up, w_down)


def solution(mesh):
    placed = (
        P(("dp", "expert"), None),
        P(("dp", "expert"), None),
        P(("dp", "expert"), None),
        P(("dp", "expert"), None),
        P("expert", "dp", None),
        P("expert", "dp", None),
        P("expert", "dp", None),
    )
    return jax.shard_map(
        body,
        mesh=mesh,
        in_specs=placed,
        out_specs=(
            P(("dp", "expert"), None),
            P("expert", "dp", None),
            P("expert", "dp", None),
            P("expert", "dp", None),
        ),
        check_vma=False,
    )
```

```python
import functools

import jax
import jax.numpy as jnp
from jax import lax
from jax.experimental import pallas as pl
from jax.experimental.pallas import tpu as pltpu
from jax.sharding import PartitionSpec as P

MESH = pl.DeviceIdType.MESH
f32 = jnp.float32
bf16 = jnp.bfloat16

D = 2048
H = 192
NX, NY, NZ = 4, 4, 16
META = 128
HALF = D // 2
PIECE = 16
PLANE = NY * PIECE
COPIES = 192

OFFSETS = (0, -1, 1, -2, 2, -3, 3, -4, 4, -5, 5, -6, 6, -7, 7, -8)
POS = {offset: place for place, offset in enumerate(OFFSETS)}


def dot_nt(a, b):
    return lax.dot_general(a, b, (((1,), (1,)), ((), ())), preferred_element_type=f32)


def dot(a, b):
    return jnp.dot(a, b, preferred_element_type=f32)


def kernel(
    tok_hbm, cot_hbm, ids_hbm, codes_hbm, wg_hbm, wu_hbm, wd_hbm,
    tg_hbm, gg_hbm, gu_hbm, gd_hbm,
    tok_ref, cot_ref, ids_ref, codes_ref, wg_ref, wu_ref, wd_ref, gz, gz_far, sel, unsel, xc, h_t, dg_t, du_t, p_own, p_sib, p_got,
    xs_o, xs_l, xs_r, xr_o, xr_l, xr_r, ys, yr, zp, zs, zr_m1, zr_m2, zr_p1, zr_p2,
    tg_ref, gg_ref, gu_ref, gd_ref,
    send_sem, recv_sem, load_sem, store_sem,
):
    me_dp = lax.axis_index("dp")
    me_e = lax.axis_index("expert")
    x, core = me_dp // 2, me_dp % 2
    y, z = me_e // NZ, me_e % NZ

    def at(dx=0, dy=0, dz=0, flip=False):
        other = (1 - core) if flip else core
        return (
            ((x + dx + NX) % NX) * 2 + other,
            ((y + dy + NY) % NY) * NZ + (z + dz + NZ) % NZ,
        )

    x_up, x_dn, x_far = at(dx=1), at(dx=-1), at(dx=2)
    z_up, z_dn, z_up2, z_dn2 = at(dz=1), at(dz=-1), at(dz=2), at(dz=-2)
    sibling = at(flip=True)
    y_peer = {1: at(dy=1), 2: at(dy=-1), 3: at(dy=2)}
    y_back = {1: at(dy=-1), 2: at(dy=1), 3: at(dy=2)}

    counter = [0]
    started = []

    def copy(src, dst, device):
        number = counter[0]
        counter[0] += 1
        made = pltpu.make_async_remote_copy(
            src_ref=src, dst_ref=dst, send_sem=send_sem.at[number],
            recv_sem=recv_sem.at[number], device_id=device, device_id_type=MESH,
        )
        started.append(made)
        made.start()
        return made

    barrier = pltpu.get_barrier_semaphore()
    partners = (z_up, z_dn, z_up2, z_dn2, at(dy=1), at(dy=-1), at(dy=2), x_up, x_dn, x_far, sibling)
    for partner in partners:
        pl.semaphore_signal(barrier, inc=1, device_id=partner, device_id_type=MESH)

    loads = [
        pltpu.make_async_copy(src, dst, load_sem.at[number])
        for number, (src, dst) in enumerate(
            ((tok_hbm, tok_ref), (cot_hbm, cot_ref), (ids_hbm, ids_ref), (codes_hbm, codes_ref),
             (wg_hbm.at[0], wg_ref), (wu_hbm.at[0], wu_ref), (wd_hbm.at[0], wd_ref))
        )
    ]
    for load in loads:
        load.start()
    for load in loads[0:4]:
        load.wait()
    rows = jnp.concatenate([tok_ref[...].astype(f32), cot_ref[...].astype(f32)], axis=0)
    gz[0, :, 0:D] = rows.astype(bf16)
    codes = codes_ref[...]
    spread_row = lax.broadcasted_iota(jnp.int32, (8, META), 0)
    spread_col = lax.broadcasted_iota(jnp.int32, (8, META), 1)
    meta = jnp.zeros((8, META), f32)
    for number, part in enumerate((ids_ref[...], codes // 8, codes % 8)):
        spread = (spread_col == spread_row + 8 * number).astype(f32)
        meta = meta + dot(part.astype(f32).astype(bf16), spread.astype(bf16))
    gz[0, :, D:D + META] = jnp.concatenate([meta, meta], axis=0).astype(bf16)
    pl.semaphore_wait(barrier, len(partners))

    cuts = ((0, HALF), (HALF, D + META - HALF))
    ring_got = {}

    def ring_send(plane, place, to_place, cut, device):
        cols = pl.ds(*cuts[cut])
        held = (gz, gz_far)[plane]
        ring_got[plane, to_place, cut] = copy(
            held.at[POS[place], :, cols], held.at[POS[to_place], :, cols], device
        )

    def ring(plane, k):
        for cut in range(2):
            for way, last, device in ((-1, 8, z_up), (1, 7, z_dn)):
                if k and k <= last:
                    ring_got[plane, way * k, cut].wait_recv()
                if k < last:
                    ring_send(plane, way * k, way * (k + 1), cut, device)

    lane = lax.broadcasted_iota(jnp.int32, (128, 128), 1)
    row = lax.broadcasted_iota(jnp.int32, (128, 128), 0)
    lane_kind, lane_dy, lane_slot = lane // 64, (lane % 64) // 16, lane % 16
    step_y = jnp.where(lane_dy == 1, 1, jnp.where(lane_dy == 2, NY - 1, jnp.where(lane_dy == 3, 2, 0)))
    lane_expert = (((y + step_y) % NY) * NZ + z).astype(f32)
    fits = (lane_kind == (row % 16) // 8) & (row // 16 == lane_slot // 2)
    earlier = ((row // 8 == lane // 8) & (lane < row)).astype(f32).astype(bf16)
    lane_rank = (lane_slot % 2).astype(f32)

    def base(c, q):
        return (c * 8 + q) * PLANE

    def select(c, plane):
        blocks = (gz, gz_far)[plane]
        to_row = base(c, 3 * plane)
        table = blocks[8 * c:8 * c + 8, :, D:D + META].reshape(128, META).astype(f32)
        hit = jnp.zeros((128, 128), f32)
        high = jnp.zeros((128, 128), f32)
        low = jnp.zeros((128, 128), f32)
        for i in range(8):
            same = table[:, i:i + 1] == lane_expert
            hit = hit + jnp.where(same, 1.0, 0.0)
            high = high + jnp.where(same, table[:, 8 + i:9 + i], 0.0)
            low = low + jnp.where(same, table[:, 16 + i:17 + i], 0.0)
        rank = dot(earlier, hit.astype(bf16))
        mine = jnp.where(fits & (rank == lane_rank), hit, 0.0)
        if plane == 0:
            unsel[c] = mine.astype(bf16)
        is_cot = lane_kind == 1
        first = (mine * jnp.where(is_cot, high * (1.0 / 128.0), 1.0)).T.astype(bf16)
        second = (mine * jnp.where(is_cot, low * (1.0 / 1024.0), 0.0)).T.astype(bf16)
        for j in range(4):
            cols = pl.ds(512 * j, 512)
            data = blocks[8 * c:8 * c + 8, :, cols].reshape(128, 512)
            got = (dot(first, data) + dot(second, data)).astype(bf16)
            for kind in range(2):
                to = pl.ds(kind * D + 512 * j, 512)
                xc[pl.ds(to_row, PIECE), to] = got[64 * kind:64 * kind + 16]
                sel[plane, c, :, :, to] = got[64 * kind + 16:64 * kind + 64].reshape(3, 16, 512)

    def y_send(c, plane):
        row = base(c, 3 * plane)
        return {
            p: copy(sel.at[plane, c, p - 1], xc.at[pl.ds(row + p * PIECE, PIECE), :], y_peer[p])
            for p in (1, 2, 3)
        }

    def piece(c, q, p):
        return xc.at[pl.ds(base(c, q) + p * PIECE, PIECE), :]

    from_dn, from_up, sib = {}, {}, {}

    def x_first(c, p):
        from_dn[c, p] = copy(piece(c, 0, p), piece(c, 1, p), x_up)
        from_up[c, p] = copy(piece(c, 0, p), piece(c, 2, p), x_dn)
        to_sibling(c, 0, p)

    def to_sibling(c, q, p):
        sib[c, q, p] = copy(piece(c, q, p), piece(c, q + 4, p), sibling)

    def x_got(c, p):
        from_dn[c, p].wait_recv()
        to_sibling(c, 1, p)
        from_up[c, p].wait_recv()
        to_sibling(c, 2, p)

    def far_y_got(c, copies):
        to_sibling(c, 3, 0)
        for p in (1, 2, 3):
            copies[p].wait_recv()
            to_sibling(c, 3, p)

    def forward(c, half):
        if half == 1:
            for q in range(4):
                for p in range(4):
                    sib[c, q, p].wait_recv()
        first = base(c, 4 * half)
        rows_here = pl.ds(first, 256)
        pre_gate = dot_nt(xc[rows_here, 0:D], wg_ref[...])
        pre_up = dot_nt(xc[rows_here, 0:D], wu_ref[...])
        d_hidden = dot_nt(xc[rows_here, D:2 * D], wd_ref[...])
        sig = jax.nn.sigmoid(pre_gate)
        active = pre_gate * sig
        hidden = active * pre_up
        d_up = d_hidden * active
        d_gate = d_hidden * pre_up * sig * (1.0 + pre_gate * (1.0 - sig))
        h_t[:, rows_here] = hidden.T.astype(bf16)
        du_t[:, rows_here] = d_up.T.astype(bf16)
        dg_t[:, rows_here] = d_gate.T.astype(bf16)
        d_up, d_gate = d_up.astype(bf16), d_gate.astype(bf16)
        into = p_sib if half else p_own
        for j in range(4):
            cols = pl.ds(512 * j, 512)
            part = dot(d_gate, wg_ref[:, cols]) + dot(d_up, wu_ref[:, cols])
            into[c, :, cols] = part.astype(bf16)

    def core_send(c):
        return {
            q: copy(p_sib.at[c, pl.ds(q * PLANE, PLANE)], p_got.at[c, pl.ds(q * PLANE, PLANE)], sibling)
            for q in (3, 2, 1, 0)
        }

    def pair(c, q, cols):
        here = pl.ds(q * PLANE, PLANE)
        return p_own[c, here, cols].astype(f32) + p_got[c, here, cols].astype(f32)

    left, right, both = pl.ds(0, HALF), pl.ds(HALF, HALF), pl.ds(0, D)

    def x_return_first(c, core_copies):
        core_copies[3].wait_recv()
        xs_o[c] = pair(c, 3, both).astype(bf16)
        relay_r = copy(xs_o.at[c, :, left], xr_o.at[c, :, left], x_up)
        relay_l = copy(xs_o.at[c, :, right], xr_o.at[c, :, right], x_dn)
        core_copies[2].wait_recv()
        xs_r[c, :, right] = pair(c, 2, right).astype(bf16)
        r_plain = copy(xs_r.at[c, :, right], xr_l.at[c, :, right], x_up)
        core_copies[1].wait_recv()
        xs_l[c, :, left] = pair(c, 1, left).astype(bf16)
        l_plain = copy(xs_l.at[c, :, left], xr_r.at[c, :, left], x_dn)
        return relay_r, relay_l, r_plain, l_plain

    def x_return_second(c, relay_r, relay_l, r_plain, l_plain):
        relay_r.wait_recv()
        xs_r[c, :, left] = (pair(c, 2, left) + xr_o[c, :, left].astype(f32)).astype(bf16)
        r_sum = copy(xs_r.at[c, :, left], xr_l.at[c, :, left], x_up)
        relay_l.wait_recv()
        xs_l[c, :, right] = (pair(c, 1, right) + xr_o[c, :, right].astype(f32)).astype(bf16)
        l_sum = copy(xs_l.at[c, :, right], xr_r.at[c, :, right], x_dn)
        return r_plain, l_plain, r_sum, l_sum

    def y_return(c, core_copies, arriving):
        core_copies[0].wait_recv()
        for one in arriving:
            one.wait_recv()
        sends = {}
        for side, cols in enumerate((left, right)):
            total = pair(c, 0, cols) + xr_l[c, :, cols].astype(f32) + xr_r[c, :, cols].astype(f32)
            total = total.astype(bf16)
            yr[c, side, 0] = total[0:PIECE]
            ys[c, side] = total[PIECE:].reshape(3, PIECE, HALF)
        for p in (3, 1, 2):
            sends[p] = copy(ys.at[c, :, p - 1], yr.at[c, :, p], y_back[p])
        return sends

    def unselect(c, y_copies):
        for p in (1, 2, 3):
            y_copies[p].wait_recv()
        part = dot(unsel[c], yr[c].reshape(128, HALF))
        zp[8 * c:8 * c + 8] = part.reshape(8, 16, HALF)

    stores = []

    def store(src, dst):
        stores.append(pltpu.make_async_copy(src, dst, store_sem.at[len(stores)]))
        stores[-1].start()

    def grad_tile(kind, j):
        out, lhs, shift = ((gg_ref, dg_t, 0), (gu_ref, du_t, 0), (gd_ref, h_t, D))[kind]
        data = xc[:, pl.ds(shift + 512 * j, 512)]
        out[:, pl.ds(512 * j, 512)] = dot(lhs[...], data).astype(bf16)
        if j == 3:
            store(out, (gg_hbm, gu_hbm, gd_hbm)[kind].at[0])

    tiles = [(kind, j) for kind in range(3) for j in range(4)]

    def some_grads(count):
        for _ in range(min(count, len(tiles))):
            grad_tile(*tiles.pop(0))

    ring(0, 0)
    raw = copy(gz.at[0], gz_far.at[0], x_far)
    ring(0, 1)
    raw.wait_recv()
    ring(1, 0)
    ring(0, 2)
    ring(1, 1)
    ring(0, 3)
    ring(1, 2)
    ring(0, 4)
    select(0, 0)
    y0 = y_send(0, 0)
    x_first(0, 0)
    ring(1, 3)
    ring(0, 5)
    ring(1, 4)
    select(0, 1)
    far_y0 = y_send(0, 1)
    ring(0, 6)
    y0[1].wait_recv()
    x_first(0, 1)
    y0[2].wait_recv()
    x_first(0, 2)
    ring(1, 5)
    y0[3].wait_recv()
    x_first(0, 3)
    ring(0, 7)
    ring(1, 6)
    x_got(0, 0)
    ring(0, 8)
    select(1, 0)
    y1 = y_send(1, 0)
    x_first(1, 0)
    ring(1, 7)
    x_got(0, 1)
    x_got(0, 2)
    ring(1, 8)
    select(1, 1)
    far_y1 = y_send(1, 1)
    x_got(0, 3)
    for p in (1, 2, 3):
        y1[p].wait_recv()
        x_first(1, p)
    far_y_got(0, far_y0)
    for load in loads[4:]:
        load.wait()
    forward(0, 1)
    core0 = core_send(0)
    forward(0, 0)
    x_got(1, 0)
    x_got(1, 1)
    x0 = x_return_first(0, core0)
    x_got(1, 2)
    x_got(1, 3)
    far_y_got(1, far_y1)
    forward(1, 1)
    core1 = core_send(1)
    forward(1, 0)
    x1 = x_return_first(1, core1)
    x0 = x_return_second(0, *x0)
    x1 = x_return_second(1, *x1)
    back0 = y_return(0, core0, x0)
    some_grads(1)
    unselect(0, back0)

    z_sum = {}

    def z_back(place, block, device, into, number):
        zs[POS[place]] = block.astype(bf16)
        z_sum[place] = copy(zs.at[POS[place]], into.at[number], device)

    def z_odd(k):
        z_back(-k, zp[POS[-k]], z_dn, zr_m1, (7 - k) // 2)
        z_back(k, zp[POS[k]], z_up, zr_p1, (7 - k) // 2)

    def z_even(k):
        number = (8 - k) // 2
        block = zp[POS[-k]]
        if k < 8:
            z_sum[-k - 2].wait_recv()
            z_sum[-k - 1].wait_recv()
            block = block + zr_m2[number - 1].astype(f32) + zr_m1[number - 1].astype(f32)
        z_back(-k, block, z_dn2, zr_m2, number)
        if k < 8:
            z_sum[k + 1].wait_recv()
            block = zp[POS[k]] + zr_p1[number - 1].astype(f32)
            if k < 6:
                z_sum[k + 2].wait_recv()
                block = block + zr_p2[number - 1].astype(f32)
            z_back(k, block, z_up2, zr_p2, number)

    z_odd(3)
    z_odd(1)
    some_grads(1)
    back1 = y_return(1, core1, x1)
    some_grads(3)
    unselect(1, back1)
    z_even(8)
    z_odd(7)
    z_odd(5)
    some_grads(2)
    z_even(6)
    some_grads(2)
    z_even(4)
    some_grads(2)
    z_even(2)
    some_grads(len(tiles))
    total = zp[0]
    for place, got in ((-1, zr_m1), (1, zr_p1), (-2, zr_m2), (2, zr_p2)):
        z_sum[place].wait_recv()
        total = total + got[3].astype(f32)
    tg_ref[:, 0:HALF] = total[0:8].astype(bf16)
    tg_ref[:, HALF:D] = total[8:16].astype(bf16)
    store(tg_ref, tg_hbm)
    for one in stores:
        one.wait()

    for made in started:
        made.wait_send()


def deliver(*refs):
    ins, outs, held, sems = refs[0:4], refs[4:8], refs[8:12], refs[12]
    fetch = [pltpu.make_async_copy(ins[i], held[i], sems.at[0, i]) for i in range(4)]
    store = [pltpu.make_async_copy(held[i], outs[i], sems.at[1, i]) for i in range(4)]
    for one in fetch:
        one.start()
    for i in range(4):
        fetch[i].wait()
        store[i].start()
    for one in store:
        one.wait()


def body(tokens, cotangent, expert_ids, gate_codes, w_gate, w_up, w_down):
    hbm = pl.BlockSpec(memory_space=pl.ANY)
    shapes = (
        jax.ShapeDtypeStruct((8, D), bf16),
        jax.ShapeDtypeStruct((1, H, D), bf16),
        jax.ShapeDtypeStruct((1, H, D), bf16),
        jax.ShapeDtypeStruct((1, H, D), bf16),
    )
    results = pl.pallas_call(
        kernel,
        out_shape=shapes,
        in_specs=[hbm] * 7,
        out_specs=(hbm,) * 4,
        scratch_shapes=[pltpu.VMEM((8, D), bf16)] * 2
        + [pltpu.VMEM((8, 8), jnp.int32)] * 2
        + [pltpu.VMEM((H, D), bf16)] * 3
        + [
            pltpu.VMEM((NZ, 16, D + META), bf16),
            pltpu.VMEM((NZ, 16, D + META), bf16),
            pltpu.VMEM((2, 2, 3, PIECE, 2 * D), bf16),
            pltpu.VMEM((2, 128, 128), bf16),
            pltpu.VMEM((1024, 2 * D), bf16),
            pltpu.VMEM((H, 1024), bf16),
            pltpu.VMEM((H, 1024), bf16),
            pltpu.VMEM((H, 1024), bf16),
            pltpu.VMEM((2, 256, D), bf16),
            pltpu.VMEM((2, 256, D), bf16),
            pltpu.VMEM((2, 256, D), bf16),
        ]
        + [pltpu.VMEM((2, PLANE, D), bf16)] * 6
        + [
            pltpu.VMEM((2, 2, 3, PIECE, HALF), bf16),
            pltpu.VMEM((2, 2, 4, PIECE, HALF), bf16),
            pltpu.VMEM((NZ, 16, HALF), f32),
            pltpu.VMEM((NZ, 16, HALF), bf16),
        ]
        + [pltpu.VMEM((4, 16, HALF), bf16)] * 4
        + [pltpu.VMEM((8, D), bf16)]
        + [pltpu.VMEM((H, D), bf16)] * 3
        + [
            pltpu.SemaphoreType.DMA((COPIES,)),
            pltpu.SemaphoreType.DMA((COPIES,)),
            pltpu.SemaphoreType.DMA((7,)),
            pltpu.SemaphoreType.DMA((4,)),
        ],
        compiler_params=pltpu.CompilerParams(
            collective_id=0, has_side_effects=True, vmem_limit_bytes=60 * 1024 * 1024
        ),
        name="expert_layer_backward",
    )(tokens, cotangent, expert_ids, gate_codes, w_gate, w_up, w_down)
    return pl.pallas_call(
        deliver,
        out_shape=shapes,
        in_specs=[hbm] * 4,
        out_specs=(hbm,) * 4,
        scratch_shapes=[pltpu.VMEM(shape.shape, bf16) for shape in shapes]
        + [pltpu.SemaphoreType.DMA((2, 4))],
        compiler_params=pltpu.CompilerParams(vmem_limit_bytes=60 * 1024 * 1024),
        name="deliver",
    )(*results)


def solution(mesh):
    placed = (
        P(("dp", "expert"), None),
        P(("dp", "expert"), None),
        P(("dp", "expert"), None),
        P(("dp", "expert"), None),
        P("expert", "dp", None),
        P("expert", "dp", None),
        P("expert", "dp", None),
    )
    return jax.shard_map(
        body,
        mesh=mesh,
        in_specs=placed,
        out_specs=(
            P(("dp", "expert"), None),
            P("expert", "dp", None),
            P("expert", "dp", None),
            P("expert", "dp", None),
        ),
        check_vma=False,
    )
```

```python
import functools

import jax
import jax.numpy as jnp
from jax import lax
from jax.experimental import pallas as pl
from jax.experimental.pallas import tpu as pltpu
from jax.sharding import PartitionSpec as P

MESH = pl.DeviceIdType.MESH
f32 = jnp.float32
bf16 = jnp.bfloat16

D = 2048
H = 192
NX, NY, NZ = 4, 4, 16
META = 128
HALF = D // 2
PIECE = 16
TILE = 512
PLANE = NY * PIECE
COPIES = 208

OFFSETS = (0, -1, 1, -2, 2, -3, 3, -4, 4, -5, 5, -6, 6, -7, 7, -8)
POS = {offset: place for place, offset in enumerate(OFFSETS)}


def dot_nt(a, b):
    return lax.dot_general(a, b, (((1,), (1,)), ((), ())), preferred_element_type=f32)


def dot(a, b):
    return jnp.dot(a, b, preferred_element_type=f32)


def kernel(
    tok_hbm, cot_hbm, ids_hbm, codes_hbm, wg_hbm, wu_hbm, wd_hbm,
    tg_hbm, gg_hbm, gu_hbm, gd_hbm,
    tok_ref, cot_ref, ids_ref, codes_ref, wg_ref, wu_ref, wd_ref, gz, gz_far, sel, unsel, xc, h_t, dg_t, du_t, p_own, p_sib, p_got,
    xs_o, xs_l, xs_r, xr_o, xr_l, xr_r, ys, yr, zp, zs, zr_m1, zr_m2, zr_p1, zr_p2,
    tg_ref, gg_ref, gu_ref, gd_ref,
    send_sem, recv_sem, load_sem, store_sem,
):
    me_dp = lax.axis_index("dp")
    me_e = lax.axis_index("expert")
    x, core = me_dp // 2, me_dp % 2
    y, z = me_e // NZ, me_e % NZ

    def at(dx=0, dy=0, dz=0, flip=False):
        other = (1 - core) if flip else core
        return (
            ((x + dx + NX) % NX) * 2 + other,
            ((y + dy + NY) % NY) * NZ + (z + dz + NZ) % NZ,
        )

    x_up, x_dn, x_far = at(dx=1), at(dx=-1), at(dx=2)
    z_up, z_dn, z_up2, z_dn2 = at(dz=1), at(dz=-1), at(dz=2), at(dz=-2)
    sibling = at(flip=True)
    y_peer = {1: at(dy=1), 2: at(dy=-1), 3: at(dy=2)}
    y_back = {1: at(dy=-1), 2: at(dy=1), 3: at(dy=2)}

    counter = [0]
    started = []

    def copy(src, dst, device):
        number = counter[0]
        counter[0] += 1
        made = pltpu.make_async_remote_copy(
            src_ref=src, dst_ref=dst, send_sem=send_sem.at[number],
            recv_sem=recv_sem.at[number], device_id=device, device_id_type=MESH,
        )
        started.append(made)
        made.start()
        return made

    barrier = pltpu.get_barrier_semaphore()
    partners = (z_up, z_dn, z_up2, z_dn2, at(dy=1), at(dy=-1), at(dy=2), x_up, x_dn, x_far, sibling)
    for partner in partners:
        pl.semaphore_signal(barrier, inc=1, device_id=partner, device_id_type=MESH)

    loads = [
        pltpu.make_async_copy(src, dst, load_sem.at[number])
        for number, (src, dst) in enumerate(
            ((tok_hbm, tok_ref), (cot_hbm, cot_ref), (ids_hbm, ids_ref), (codes_hbm, codes_ref),
             (wg_hbm.at[0], wg_ref), (wu_hbm.at[0], wu_ref), (wd_hbm.at[0], wd_ref))
        )
    ]
    for load in loads:
        load.start()
    for load in loads[0:4]:
        load.wait()
    rows = jnp.concatenate([tok_ref[...].astype(f32), cot_ref[...].astype(f32)], axis=0)
    gz[0, :, 0:D] = rows.astype(bf16)
    codes = codes_ref[...]
    spread_row = lax.broadcasted_iota(jnp.int32, (8, META), 0)
    spread_col = lax.broadcasted_iota(jnp.int32, (8, META), 1)
    meta = jnp.zeros((8, META), f32)
    for number, part in enumerate((ids_ref[...], codes // 8, codes % 8)):
        spread = (spread_col == spread_row + 8 * number).astype(f32)
        meta = meta + dot(part.astype(f32).astype(bf16), spread.astype(bf16))
    gz[0, :, D:D + META] = jnp.concatenate([meta, meta], axis=0).astype(bf16)
    pl.semaphore_wait(barrier, len(partners))

    cuts = ((0, HALF), (HALF, D + META - HALF))
    ring_got = {}

    def ring_send(plane, place, to_place, cut, device):
        cols = pl.ds(*cuts[cut])
        held = (gz, gz_far)[plane]
        ring_got[plane, to_place, cut] = copy(
            held.at[POS[place], :, cols], held.at[POS[to_place], :, cols], device
        )

    def ring(plane, k):
        for cut in range(2):
            for way, last, device in ((-1, 8, z_up), (1, 7, z_dn)):
                if k and k <= last:
                    ring_got[plane, way * k, cut].wait_recv()
                if k < last:
                    ring_send(plane, way * k, way * (k + 1), cut, device)

    lane = lax.broadcasted_iota(jnp.int32, (128, 128), 1)
    row = lax.broadcasted_iota(jnp.int32, (128, 128), 0)
    lane_kind, lane_dy, lane_slot = lane // 64, (lane % 64) // 16, lane % 16
    step_y = jnp.where(lane_dy == 1, 1, jnp.where(lane_dy == 2, NY - 1, jnp.where(lane_dy == 3, 2, 0)))
    lane_expert = (((y + step_y) % NY) * NZ + z).astype(f32)
    fits = (lane_kind == (row % 16) // 8) & (row // 16 == lane_slot // 2)
    earlier = ((row // 8 == lane // 8) & (lane < row)).astype(f32).astype(bf16)
    lane_rank = (lane_slot % 2).astype(f32)

    def base(c, q):
        return (c * 8 + q) * PLANE

    def select(c, plane):
        blocks = (gz, gz_far)[plane]
        to_row = base(c, 3 * plane)
        table = blocks[8 * c:8 * c + 8, :, D:D + META].reshape(128, META).astype(f32)
        hit = jnp.zeros((128, 128), f32)
        high = jnp.zeros((128, 128), f32)
        low = jnp.zeros((128, 128), f32)
        for i in range(8):
            same = table[:, i:i + 1] == lane_expert
            hit = hit + jnp.where(same, 1.0, 0.0)
            high = high + jnp.where(same, table[:, 8 + i:9 + i], 0.0)
            low = low + jnp.where(same, table[:, 16 + i:17 + i], 0.0)
        rank = dot(earlier, hit.astype(bf16))
        mine = jnp.where(fits & (rank == lane_rank), hit, 0.0)
        if plane == 0:
            unsel[c] = mine.astype(bf16)
        is_cot = lane_kind == 1
        first = (mine * jnp.where(is_cot, high * (1.0 / 128.0), 1.0)).T.astype(bf16)
        second = (mine * jnp.where(is_cot, low * (1.0 / 1024.0), 0.0)).T.astype(bf16)
        for j in range(4):
            cols = pl.ds(512 * j, 512)
            data = blocks[8 * c:8 * c + 8, :, cols].reshape(128, 512)
            got = (dot(first, data) + dot(second, data)).astype(bf16)
            for kind in range(2):
                to = pl.ds(kind * D + 512 * j, 512)
                xc[pl.ds(to_row, PIECE), to] = got[64 * kind:64 * kind + 16]
                sel[plane, c, :, :, to] = got[64 * kind + 16:64 * kind + 64].reshape(3, 16, 512)

    def y_send(c, plane):
        row = base(c, 3 * plane)
        return {
            p: copy(sel.at[plane, c, p - 1], xc.at[pl.ds(row + p * PIECE, PIECE), :], y_peer[p])
            for p in (1, 2, 3)
        }

    def piece(c, q, p):
        return xc.at[pl.ds(base(c, q) + p * PIECE, PIECE), :]

    from_dn, from_up, sib = {}, {}, {}

    def x_first(c, p):
        from_dn[c, p] = copy(piece(c, 0, p), piece(c, 1, p), x_up)
        from_up[c, p] = copy(piece(c, 0, p), piece(c, 2, p), x_dn)
        to_sibling(c, 0, p)

    def to_sibling(c, q, p):
        sib[c, q, p] = copy(piece(c, q, p), piece(c, q + 4, p), sibling)

    def x_got(c, p):
        from_dn[c, p].wait_recv()
        to_sibling(c, 1, p)
        from_up[c, p].wait_recv()
        to_sibling(c, 2, p)

    def far_y_got(c, copies):
        to_sibling(c, 3, 0)
        for p in (1, 2, 3):
            copies[p].wait_recv()
            to_sibling(c, 3, p)

    def forward(c, half):
        if half == 1:
            for q in range(4):
                for p in range(4):
                    sib[c, q, p].wait_recv()
        rows_here = pl.ds(base(c, 4 * half), 256)
        pre_gate = dot_nt(xc[rows_here, 0:D], wg_ref[...])
        pre_up = dot_nt(xc[rows_here, 0:D], wu_ref[...])
        d_hidden = dot_nt(xc[rows_here, D:2 * D], wd_ref[...])
        sig = jax.nn.sigmoid(pre_gate)
        active = pre_gate * sig
        hidden = active * pre_up
        d_up = d_hidden * active
        d_gate = d_hidden * pre_up * sig * (1.0 + pre_gate * (1.0 - sig))
        h_t[:, rows_here] = hidden.T.astype(bf16)
        du_t[:, rows_here] = d_up.T.astype(bf16)
        dg_t[:, rows_here] = d_gate.T.astype(bf16)
        return d_gate.astype(bf16), d_up.astype(bf16)

    def tile(j):
        return pl.ds(TILE * j, TILE)

    def forward_tile(c, half, d_gate, d_up, j):
        into = p_sib if half else p_own
        part = dot(d_gate, wg_ref[:, tile(j)]) + dot(d_up, wu_ref[:, tile(j)])
        into[c, :, tile(j)] = part.astype(bf16)

    core = {}

    def forward_sibling(c):
        d_gate, d_up = forward(c, 1)
        for j in (0, 2, 1, 3):
            forward_tile(c, 1, d_gate, d_up, j)
            core[c, j] = copy(p_sib.at[c, :, tile(j)], p_got.at[c, :, tile(j)], sibling)

    def pair(c, q, j):
        here = pl.ds(q * PLANE, PLANE)
        return p_own[c, here, tile(j)].astype(f32) + p_got[c, here, tile(j)].astype(f32)

    back_x = {}

    def x_return_first(c, g):
        left, right = g, 2 + g
        core[c, left].wait_recv()
        xs_o[c, :, tile(left)] = pair(c, 3, left).astype(bf16)
        relay_r = copy(xs_o.at[c, :, tile(left)], xr_o.at[c, :, tile(left)], x_up)
        xs_l[c, :, tile(left)] = pair(c, 1, left).astype(bf16)
        l_plain = copy(xs_l.at[c, :, tile(left)], xr_r.at[c, :, tile(left)], x_dn)
        core[c, right].wait_recv()
        xs_o[c, :, tile(right)] = pair(c, 3, right).astype(bf16)
        relay_l = copy(xs_o.at[c, :, tile(right)], xr_o.at[c, :, tile(right)], x_dn)
        xs_r[c, :, tile(right)] = pair(c, 2, right).astype(bf16)
        r_plain = copy(xs_r.at[c, :, tile(right)], xr_l.at[c, :, tile(right)], x_up)
        back_x[c, g] = [relay_r, relay_l, l_plain, r_plain]

    def x_return_second(c, g):
        left, right = g, 2 + g
        relay_r, relay_l, l_plain, r_plain = back_x[c, g]
        relay_r.wait_recv()
        xs_r[c, :, tile(left)] = (pair(c, 2, left) + xr_o[c, :, tile(left)].astype(f32)).astype(bf16)
        r_sum = copy(xs_r.at[c, :, tile(left)], xr_l.at[c, :, tile(left)], x_up)
        relay_l.wait_recv()
        xs_l[c, :, tile(right)] = (pair(c, 1, right) + xr_o[c, :, tile(right)].astype(f32)).astype(bf16)
        l_sum = copy(xs_l.at[c, :, tile(right)], xr_r.at[c, :, tile(right)], x_dn)
        back_x[c, g] = [l_plain, r_plain, r_sum, l_sum]

    back_y = {}

    def y_return(c, g):
        for one in back_x[c, g]:
            one.wait_recv()
        for side in range(2):
            j = 2 * side + g
            total = pair(c, 0, j) + xr_l[c, :, tile(j)].astype(f32) + xr_r[c, :, tile(j)].astype(f32)
            total = total.astype(bf16)
            yr[c, side, 0, :, tile(g)] = total[0:PIECE]
            ys[c, side, :, :, tile(g)] = total[PIECE:].reshape(3, PIECE, TILE)
        for p in (3, 1, 2):
            back_y[c, g, p] = copy(
                ys.at[c, :, p - 1, :, tile(g)], yr.at[c, :, p, :, tile(g)], y_back[p]
            )

    def unselect(c, g):
        for p in (1, 2, 3):
            back_y[c, g, p].wait_recv()
        part = dot(unsel[c], yr[c, :, :, :, tile(g)].reshape(128, TILE))
        zp[8 * c:8 * c + 8, :, tile(g)] = part.reshape(8, 16, TILE)

    z_sum = {}

    def z_back(place, g, block, device, into, number):
        zs[POS[place], :, tile(g)] = block.astype(bf16)
        z_sum[place, g] = copy(
            zs.at[POS[place], :, tile(g)], into.at[number, :, tile(g)], device
        )

    def z_odd(k, g):
        z_back(-k, g, zp[POS[-k], :, tile(g)], z_dn, zr_m1, (7 - k) // 2)
        z_back(k, g, zp[POS[k], :, tile(g)], z_up, zr_p1, (7 - k) // 2)

    def z_even(k, g):
        number = (8 - k) // 2
        block = zp[POS[-k], :, tile(g)]
        if k < 8:
            z_sum[-k - 2, g].wait_recv()
            z_sum[-k - 1, g].wait_recv()
            block = block + zr_m2[number - 1, :, tile(g)].astype(f32)
            block = block + zr_m1[number - 1, :, tile(g)].astype(f32)
        z_back(-k, g, block, z_dn2, zr_m2, number)
        if k < 8:
            z_sum[k + 1, g].wait_recv()
            block = zp[POS[k], :, tile(g)] + zr_p1[number - 1, :, tile(g)].astype(f32)
            if k < 6:
                z_sum[k + 2, g].wait_recv()
                block = block + zr_p2[number - 1, :, tile(g)].astype(f32)
            z_back(k, g, block, z_up2, zr_p2, number)

    def z_last(g):
        total = zp[0, :, tile(g)]
        for place, got in ((-1, zr_m1), (1, zr_p1), (-2, zr_m2), (2, zr_p2)):
            z_sum[place, g].wait_recv()
            total = total + got[3, :, tile(g)].astype(f32)
        tg_ref[:, tile(g)] = total[0:8].astype(bf16)
        tg_ref[:, tile(2 + g)] = total[8:16].astype(bf16)

    stores = []

    def store(src, dst):
        stores.append(pltpu.make_async_copy(src, dst, store_sem.at[len(stores)]))
        stores[-1].start()

    def grad_tile(kind, j):
        out, lhs, shift = ((gg_ref, dg_t, 0), (gu_ref, du_t, 0), (gd_ref, h_t, D))[kind]
        data = xc[:, pl.ds(shift + 512 * j, 512)]
        out[:, pl.ds(512 * j, 512)] = dot(lhs[...], data).astype(bf16)
        if j == 3:
            store(out, (gg_hbm, gu_hbm, gd_hbm)[kind].at[0])

    tiles = [(kind, j) for kind in range(3) for j in range(4)]

    def some_grads(count):
        for _ in range(min(count, len(tiles))):
            grad_tile(*tiles.pop(0))

    ring(0, 0)
    raw = copy(gz.at[0], gz_far.at[0], x_far)
    ring(0, 1)
    raw.wait_recv()
    ring(1, 0)
    ring(0, 2)
    ring(1, 1)
    ring(0, 3)
    ring(1, 2)
    ring(0, 4)
    select(0, 0)
    y0 = y_send(0, 0)
    x_first(0, 0)
    ring(1, 3)
    ring(0, 5)
    ring(1, 4)
    select(0, 1)
    far_y0 = y_send(0, 1)
    ring(0, 6)
    y0[1].wait_recv()
    x_first(0, 1)
    y0[2].wait_recv()
    x_first(0, 2)
    ring(1, 5)
    y0[3].wait_recv()
    x_first(0, 3)
    ring(0, 7)
    x_got(0, 0)
    ring(1, 6)
    x_got(0, 1)
    ring(0, 8)
    select(1, 0)
    y1 = y_send(1, 0)
    x_first(1, 0)
    ring(1, 7)
    far_y_got(0, far_y0)
    x_got(0, 2)
    x_got(0, 3)
    for load in loads[4:]:
        load.wait()
    own0 = forward(0, 0)
    ring(1, 8)
    select(1, 1)
    far_y1 = y_send(1, 1)
    for p in (1, 2):
        y1[p].wait_recv()
        x_first(1, p)
    forward_sibling(0)
    y1[3].wait_recv()
    x_first(1, 3)
    for j in (0, 2, 1, 3):
        forward_tile(0, 0, *own0, j)
    x_got(1, 0)
    x_return_first(0, 0)
    x_return_first(0, 1)
    x_got(1, 1)
    x_got(1, 2)
    x_got(1, 3)
    far_y_got(1, far_y1)

    forward_sibling(1)
    own1 = forward(1, 0)
    forward_tile(1, 0, *own1, 0)
    forward_tile(1, 0, *own1, 2)
    x_return_first(1, 0)
    forward_tile(1, 0, *own1, 1)
    forward_tile(1, 0, *own1, 3)
    x_return_first(1, 1)
    x_return_second(0, 0)
    x_return_second(0, 1)
    x_return_second(1, 0)
    x_return_second(1, 1)
    y_return(0, 0)
    y_return(0, 1)
    some_grads(1)
    y_return(1, 0)
    y_return(1, 1)
    for g in range(2):
        unselect(0, g)
        z_odd(3, g)
        z_odd(1, g)
    some_grads(1)
    for g in range(2):
        unselect(1, g)
        z_even(8, g)
        z_odd(7, g)
        z_odd(5, g)
        some_grads(1)
    for k in (6, 4, 2):
        for g in range(2):
            z_even(k, g)
            some_grads(1)
    some_grads(len(tiles))
    for g in range(2):
        z_last(g)
    store(tg_ref, tg_hbm)
    for one in stores:
        one.wait()

    for made in started:
        made.wait_send()


def deliver(*refs):
    ins, outs, held, sems = refs[0:4], refs[4:8], refs[8:12], refs[12]
    fetch = [pltpu.make_async_copy(ins[i], held[i], sems.at[0, i]) for i in range(4)]
    store = [pltpu.make_async_copy(held[i], outs[i], sems.at[1, i]) for i in range(4)]
    for one in fetch:
        one.start()
    for i in range(4):
        fetch[i].wait()
        store[i].start()
    for one in store:
        one.wait()


def body(tokens, cotangent, expert_ids, gate_codes, w_gate, w_up, w_down):
    hbm = pl.BlockSpec(memory_space=pl.ANY)
    shapes = (
        jax.ShapeDtypeStruct((8, D), bf16),
        jax.ShapeDtypeStruct((1, H, D), bf16),
        jax.ShapeDtypeStruct((1, H, D), bf16),
        jax.ShapeDtypeStruct((1, H, D), bf16),
    )
    results = pl.pallas_call(
        kernel,
        out_shape=shapes,
        in_specs=[hbm] * 7,
        out_specs=(hbm,) * 4,
        scratch_shapes=[pltpu.VMEM((8, D), bf16)] * 2
        + [pltpu.VMEM((8, 8), jnp.int32)] * 2
        + [pltpu.VMEM((H, D), bf16)] * 3
        + [
            pltpu.VMEM((NZ, 16, D + META), bf16),
            pltpu.VMEM((NZ, 16, D + META), bf16),
            pltpu.VMEM((2, 2, 3, PIECE, 2 * D), bf16),
            pltpu.VMEM((2, 128, 128), bf16),
            pltpu.VMEM((1024, 2 * D), bf16),
            pltpu.VMEM((H, 1024), bf16),
            pltpu.VMEM((H, 1024), bf16),
            pltpu.VMEM((H, 1024), bf16),
            pltpu.VMEM((2, 256, D), bf16),
            pltpu.VMEM((2, 256, D), bf16),
            pltpu.VMEM((2, 256, D), bf16),
        ]
        + [pltpu.VMEM((2, PLANE, D), bf16)] * 6
        + [
            pltpu.VMEM((2, 2, 3, PIECE, HALF), bf16),
            pltpu.VMEM((2, 2, 4, PIECE, HALF), bf16),
            pltpu.VMEM((NZ, 16, HALF), f32),
            pltpu.VMEM((NZ, 16, HALF), bf16),
        ]
        + [pltpu.VMEM((4, 16, HALF), bf16)] * 4
        + [pltpu.VMEM((8, D), bf16)]
        + [pltpu.VMEM((H, D), bf16)] * 3
        + [
            pltpu.SemaphoreType.DMA((COPIES,)),
            pltpu.SemaphoreType.DMA((COPIES,)),
            pltpu.SemaphoreType.DMA((7,)),
            pltpu.SemaphoreType.DMA((4,)),
        ],
        compiler_params=pltpu.CompilerParams(
            collective_id=0, has_side_effects=True, vmem_limit_bytes=60 * 1024 * 1024
        ),
        name="expert_layer_backward",
    )(tokens, cotangent, expert_ids, gate_codes, w_gate, w_up, w_down)
    return pl.pallas_call(
        deliver,
        out_shape=shapes,
        in_specs=[hbm] * 4,
        out_specs=(hbm,) * 4,
        scratch_shapes=[pltpu.VMEM(shape.shape, bf16) for shape in shapes]
        + [pltpu.SemaphoreType.DMA((2, 4))],
        compiler_params=pltpu.CompilerParams(vmem_limit_bytes=60 * 1024 * 1024),
        name="deliver",
    )(*results)


def solution(mesh):
    placed = (
        P(("dp", "expert"), None),
        P(("dp", "expert"), None),
        P(("dp", "expert"), None),
        P(("dp", "expert"), None),
        P("expert", "dp", None),
        P("expert", "dp", None),
        P("expert", "dp", None),
    )
    return jax.shard_map(
        body,
        mesh=mesh,
        in_specs=placed,
        out_specs=(
            P(("dp", "expert"), None),
            P("expert", "dp", None),
            P("expert", "dp", None),
            P("expert", "dp", None),
        ),
        check_vma=False,
    )
```

```python
import functools

import jax
import jax.numpy as jnp
from jax import lax
from jax.experimental import pallas as pl
from jax.experimental.pallas import tpu as pltpu
from jax.sharding import PartitionSpec as P

MESH = pl.DeviceIdType.MESH
f32 = jnp.float32
bf16 = jnp.bfloat16

D = 2048
H = 192
NX, NY, NZ = 4, 4, 16
META = 128
HALF = D // 2
PIECE = 16
TILE = 512
PLANE = NY * PIECE
COPIES = 208

OFFSETS = (0, -1, 1, -2, 2, -3, 3, -4, 4, -5, 5, -6, 6, -7, 7, -8)
POS = {offset: place for place, offset in enumerate(OFFSETS)}


def dot_nt(a, b):
    return lax.dot_general(a, b, (((1,), (1,)), ((), ())), preferred_element_type=f32)


def dot(a, b):
    return jnp.dot(a, b, preferred_element_type=f32)


def kernel(
    tok_hbm, cot_hbm, ids_hbm, codes_hbm, wg_hbm, wu_hbm, wd_hbm,
    tg_hbm, gg_hbm, gu_hbm, gd_hbm,
    tok_ref, cot_ref, ids_ref, codes_ref, wg_ref, wu_ref, wd_ref, gz, gz_far, sel, unsel, xc, h_t, dg_t, du_t, p_own, p_sib, p_got,
    xs_o, xs_l, xs_r, xr_o, xr_l, xr_r, ys, yr, zp, zs, zr_m1, zr_m2, zr_p1, zr_p2,
    tg_ref, gg_ref, gu_ref, gd_ref,
    send_sem, recv_sem, load_sem, store_sem,
):
    me_dp = lax.axis_index("dp")
    me_e = lax.axis_index("expert")
    x, core = me_dp // 2, me_dp % 2
    y, z = me_e // NZ, me_e % NZ

    def at(dx=0, dy=0, dz=0, flip=False):
        other = (1 - core) if flip else core
        return (
            ((x + dx + NX) % NX) * 2 + other,
            ((y + dy + NY) % NY) * NZ + (z + dz + NZ) % NZ,
        )

    x_up, x_dn, x_far = at(dx=1), at(dx=-1), at(dx=2)
    z_up, z_dn, z_up2, z_dn2 = at(dz=1), at(dz=-1), at(dz=2), at(dz=-2)
    sibling = at(flip=True)
    y_peer = {1: at(dy=1), 2: at(dy=-1), 3: at(dy=2)}
    y_back = {1: at(dy=-1), 2: at(dy=1), 3: at(dy=2)}

    counter = [0]
    started = []

    def copy(src, dst, device):
        number = counter[0]
        counter[0] += 1
        made = pltpu.make_async_remote_copy(
            src_ref=src, dst_ref=dst, send_sem=send_sem.at[number],
            recv_sem=recv_sem.at[number], device_id=device, device_id_type=MESH,
        )
        started.append(made)
        made.start()
        return made

    barrier = pltpu.get_barrier_semaphore()
    partners = (z_up, z_dn, z_up2, z_dn2, at(dy=1), at(dy=-1), at(dy=2), x_up, x_dn, x_far, sibling)
    for partner in partners:
        pl.semaphore_signal(barrier, inc=1, device_id=partner, device_id_type=MESH)

    loads = [
        pltpu.make_async_copy(src, dst, load_sem.at[number])
        for number, (src, dst) in enumerate(
            ((tok_hbm, tok_ref), (cot_hbm, cot_ref), (ids_hbm, ids_ref), (codes_hbm, codes_ref),
             (wg_hbm.at[0], wg_ref), (wu_hbm.at[0], wu_ref), (wd_hbm.at[0], wd_ref))
        )
    ]
    for load in loads:
        load.start()
    for load in loads[0:4]:
        load.wait()
    rows = jnp.concatenate([tok_ref[...].astype(f32), cot_ref[...].astype(f32)], axis=0)
    gz[0, :, 0:D] = rows.astype(bf16)
    codes = codes_ref[...]
    spread_row = lax.broadcasted_iota(jnp.int32, (8, META), 0)
    spread_col = lax.broadcasted_iota(jnp.int32, (8, META), 1)
    meta = jnp.zeros((8, META), f32)
    for number, part in enumerate((ids_ref[...], codes // 8, codes % 8)):
        spread = (spread_col == spread_row + 8 * number).astype(f32)
        meta = meta + dot(part.astype(f32).astype(bf16), spread.astype(bf16))
    gz[0, :, D:D + META] = jnp.concatenate([meta, meta], axis=0).astype(bf16)
    pl.semaphore_wait(barrier, len(partners))

    cuts = ((0, HALF), (HALF, D + META - HALF))
    ring_got = {}

    def ring_send(plane, place, to_place, cut, device):
        cols = pl.ds(*cuts[cut])
        held = (gz, gz_far)[plane]
        ring_got[plane, to_place, cut] = copy(
            held.at[POS[place], :, cols], held.at[POS[to_place], :, cols], device
        )

    def ring(plane, k):
        for cut in range(2):
            for way, last, device in ((-1, 8, z_up), (1, 7, z_dn)):
                if k and k <= last:
                    ring_got[plane, way * k, cut].wait_recv()
                if k < last:
                    ring_send(plane, way * k, way * (k + 1), cut, device)

    lane = lax.broadcasted_iota(jnp.int32, (128, 128), 1)
    row = lax.broadcasted_iota(jnp.int32, (128, 128), 0)
    lane_kind, lane_dy, lane_slot = lane // 64, (lane % 64) // 16, lane % 16
    step_y = jnp.where(lane_dy == 1, 1, jnp.where(lane_dy == 2, NY - 1, jnp.where(lane_dy == 3, 2, 0)))
    lane_expert = (((y + step_y) % NY) * NZ + z).astype(f32)
    fits = (lane_kind == (row % 16) // 8) & (row // 16 == lane_slot // 2)
    earlier = ((row // 8 == lane // 8) & (lane < row)).astype(f32).astype(bf16)
    lane_rank = (lane_slot % 2).astype(f32)

    def base(c, q):
        return (c * 8 + q) * PLANE

    def select(c, plane):
        blocks = (gz, gz_far)[plane]
        to_row = base(c, 3 * plane)
        table = blocks[8 * c:8 * c + 8, :, D:D + META].reshape(128, META).astype(f32)
        hit = jnp.zeros((128, 128), f32)
        high = jnp.zeros((128, 128), f32)
        low = jnp.zeros((128, 128), f32)
        for i in range(8):
            same = table[:, i:i + 1] == lane_expert
            hit = hit + jnp.where(same, 1.0, 0.0)
            high = high + jnp.where(same, table[:, 8 + i:9 + i], 0.0)
            low = low + jnp.where(same, table[:, 16 + i:17 + i], 0.0)
        rank = dot(earlier, hit.astype(bf16))
        mine = jnp.where(fits & (rank == lane_rank), hit, 0.0)
        if plane == 0:
            unsel[c] = mine.astype(bf16)
        is_cot = lane_kind == 1
        first = (mine * jnp.where(is_cot, high * (1.0 / 128.0), 1.0)).T.astype(bf16)
        second = (mine * jnp.where(is_cot, low * (1.0 / 1024.0), 0.0)).T.astype(bf16)
        for j in range(4):
            cols = pl.ds(512 * j, 512)
            data = blocks[8 * c:8 * c + 8, :, cols].reshape(128, 512)
            got = (dot(first, data) + dot(second, data)).astype(bf16)
            for kind in range(2):
                to = pl.ds(kind * D + 512 * j, 512)
                xc[pl.ds(to_row, PIECE), to] = got[64 * kind:64 * kind + 16]
                sel[plane, c, :, :, to] = got[64 * kind + 16:64 * kind + 64].reshape(3, 16, 512)

    def y_send(c, plane):
        row = base(c, 3 * plane)
        return {
            p: copy(sel.at[plane, c, p - 1], xc.at[pl.ds(row + p * PIECE, PIECE), :], y_peer[p])
            for p in (1, 2, 3)
        }

    def piece(c, q, p):
        return xc.at[pl.ds(base(c, q) + p * PIECE, PIECE), :]

    from_dn, from_up, sib = {}, {}, {}

    def x_first(c, p):
        from_dn[c, p] = copy(piece(c, 0, p), piece(c, 1, p), x_up)
        from_up[c, p] = copy(piece(c, 0, p), piece(c, 2, p), x_dn)
        to_sibling(c, 0, p)

    def to_sibling(c, q, p):
        sib[c, q, p] = copy(piece(c, q, p), piece(c, q + 4, p), sibling)

    def x_got(c, p):
        from_dn[c, p].wait_recv()
        to_sibling(c, 1, p)
        from_up[c, p].wait_recv()
        to_sibling(c, 2, p)

    def far_y_got(c, copies):
        to_sibling(c, 3, 0)
        for p in (1, 2, 3):
            copies[p].wait_recv()
            to_sibling(c, 3, p)

    def forward(c, half):
        if half == 1:
            for q in range(4):
                for p in range(4):
                    sib[c, q, p].wait_recv()
        rows_here = pl.ds(base(c, 4 * half), 256)
        pre_gate = dot_nt(xc[rows_here, 0:D], wg_ref[...])
        pre_up = dot_nt(xc[rows_here, 0:D], wu_ref[...])
        d_hidden = dot_nt(xc[rows_here, D:2 * D], wd_ref[...])
        sig = jax.nn.sigmoid(pre_gate)
        active = pre_gate * sig
        hidden = active * pre_up
        d_up = d_hidden * active
        d_gate = d_hidden * pre_up * sig * (1.0 + pre_gate * (1.0 - sig))
        h_t[:, rows_here] = hidden.T.astype(bf16)
        du_t[:, rows_here] = d_up.T.astype(bf16)
        dg_t[:, rows_here] = d_gate.T.astype(bf16)
        return d_gate.astype(bf16), d_up.astype(bf16)

    def tile(j):
        return pl.ds(TILE * j, TILE)

    def forward_tile(c, half, d_gate, d_up, j):
        into = p_sib if half else p_own
        part = dot(d_gate, wg_ref[:, tile(j)]) + dot(d_up, wu_ref[:, tile(j)])
        into[c, :, tile(j)] = part.astype(bf16)

    core = {}

    def forward_sibling(c):
        d_gate, d_up = forward(c, 1)
        for j in (0, 2, 1, 3):
            forward_tile(c, 1, d_gate, d_up, j)
            core[c, j] = copy(p_sib.at[c, :, tile(j)], p_got.at[c, :, tile(j)], sibling)

    def pair(c, q, j):
        here = pl.ds(q * PLANE, PLANE)
        return p_own[c, here, tile(j)].astype(f32) + p_got[c, here, tile(j)].astype(f32)

    back_x = {}

    def x_return_first(c, g):
        left, right = g, 2 + g
        core[c, left].wait_recv()
        xs_o[c, :, tile(left)] = pair(c, 3, left).astype(bf16)
        relay_r = copy(xs_o.at[c, :, tile(left)], xr_o.at[c, :, tile(left)], x_up)
        xs_l[c, :, tile(left)] = pair(c, 1, left).astype(bf16)
        l_plain = copy(xs_l.at[c, :, tile(left)], xr_r.at[c, :, tile(left)], x_dn)
        core[c, right].wait_recv()
        xs_o[c, :, tile(right)] = pair(c, 3, right).astype(bf16)
        relay_l = copy(xs_o.at[c, :, tile(right)], xr_o.at[c, :, tile(right)], x_dn)
        xs_r[c, :, tile(right)] = pair(c, 2, right).astype(bf16)
        r_plain = copy(xs_r.at[c, :, tile(right)], xr_l.at[c, :, tile(right)], x_up)
        back_x[c, g] = [relay_r, relay_l, l_plain, r_plain]

    def x_return_second(c, g):
        left, right = g, 2 + g
        relay_r, relay_l, l_plain, r_plain = back_x[c, g]
        relay_r.wait_recv()
        xs_r[c, :, tile(left)] = (pair(c, 2, left) + xr_o[c, :, tile(left)].astype(f32)).astype(bf16)
        r_sum = copy(xs_r.at[c, :, tile(left)], xr_l.at[c, :, tile(left)], x_up)
        relay_l.wait_recv()
        xs_l[c, :, tile(right)] = (pair(c, 1, right) + xr_o[c, :, tile(right)].astype(f32)).astype(bf16)
        l_sum = copy(xs_l.at[c, :, tile(right)], xr_r.at[c, :, tile(right)], x_dn)
        back_x[c, g] = [l_plain, r_plain, r_sum, l_sum]

    back_y = {}

    def y_return(c, g):
        for one in back_x[c, g]:
            one.wait_recv()
        for side in range(2):
            j = 2 * side + g
            total = pair(c, 0, j) + xr_l[c, :, tile(j)].astype(f32) + xr_r[c, :, tile(j)].astype(f32)
            total = total.astype(bf16)
            yr[c, side, 0, :, tile(g)] = total[0:PIECE]
            ys[c, side, :, :, tile(g)] = total[PIECE:].reshape(3, PIECE, TILE)
        for p in (3, 1, 2):
            back_y[c, g, p] = copy(
                ys.at[c, :, p - 1, :, tile(g)], yr.at[c, :, p, :, tile(g)], y_back[p]
            )

    def unselect(c, g):
        for p in (1, 2, 3):
            back_y[c, g, p].wait_recv()
        part = dot(unsel[c], yr[c, :, :, :, tile(g)].reshape(128, TILE))
        zp[8 * c:8 * c + 8, :, tile(g)] = part.reshape(8, 16, TILE)

    z_sum = {}

    def z_back(place, g, block, device, into, number):
        zs[POS[place], :, tile(g)] = block.astype(bf16)
        z_sum[place, g] = copy(
            zs.at[POS[place], :, tile(g)], into.at[number, :, tile(g)], device
        )

    def z_odd(k, g):
        z_back(-k, g, zp[POS[-k], :, tile(g)], z_dn, zr_m1, (7 - k) // 2)
        z_back(k, g, zp[POS[k], :, tile(g)], z_up, zr_p1, (7 - k) // 2)

    def z_even(k, g):
        number = (8 - k) // 2
        block = zp[POS[-k], :, tile(g)]
        if k < 8:
            z_sum[-k - 2, g].wait_recv()
            z_sum[-k - 1, g].wait_recv()
            block = block + zr_m2[number - 1, :, tile(g)].astype(f32)
            block = block + zr_m1[number - 1, :, tile(g)].astype(f32)
        z_back(-k, g, block, z_dn2, zr_m2, number)
        if k < 8:
            z_sum[k + 1, g].wait_recv()
            block = zp[POS[k], :, tile(g)] + zr_p1[number - 1, :, tile(g)].astype(f32)
            if k < 6:
                z_sum[k + 2, g].wait_recv()
                block = block + zr_p2[number - 1, :, tile(g)].astype(f32)
            z_back(k, g, block, z_up2, zr_p2, number)

    def z_last(g):
        total = zp[0, :, tile(g)]
        for place, got in ((-1, zr_m1), (1, zr_p1), (-2, zr_m2), (2, zr_p2)):
            z_sum[place, g].wait_recv()
            total = total + got[3, :, tile(g)].astype(f32)
        tg_ref[:, tile(g)] = total[0:8].astype(bf16)
        tg_ref[:, tile(2 + g)] = total[8:16].astype(bf16)

    stores = []

    def store(src, dst):
        stores.append(pltpu.make_async_copy(src, dst, store_sem.at[len(stores)]))
        stores[-1].start()

    def grad_tile(kind, j):
        out, lhs, shift = ((gg_ref, dg_t, 0), (gu_ref, du_t, 0), (gd_ref, h_t, D))[kind]
        data = xc[:, pl.ds(shift + 512 * j, 512)]
        out[:, pl.ds(512 * j, 512)] = dot(lhs[...], data).astype(bf16)
        if j == 3:
            store(out, (gg_hbm, gu_hbm, gd_hbm)[kind].at[0])

    tiles = [(kind, j) for kind in range(3) for j in range(4)]

    def some_grads(count):
        for _ in range(min(count, len(tiles))):
            grad_tile(*tiles.pop(0))

    raw = copy(gz.at[0], gz_far.at[0], x_far)
    ring(0, 0)
    ring(0, 1)
    raw.wait_recv()
    ring(1, 0)
    ring(0, 2)
    ring(1, 1)
    ring(0, 3)
    ring(1, 2)
    ring(0, 4)
    select(0, 0)
    y0 = y_send(0, 0)
    x_first(0, 0)
    ring(1, 3)
    ring(0, 5)
    ring(1, 4)
    select(0, 1)
    far_y0 = y_send(0, 1)
    ring(0, 6)
    y0[1].wait_recv()
    x_first(0, 1)
    y0[2].wait_recv()
    x_first(0, 2)
    ring(1, 5)
    y0[3].wait_recv()
    x_first(0, 3)
    ring(0, 7)
    x_got(0, 0)
    ring(1, 6)
    x_got(0, 1)
    ring(0, 8)
    select(1, 0)
    y1 = y_send(1, 0)
    x_first(1, 0)
    ring(1, 7)
    far_y_got(0, far_y0)
    x_got(0, 2)
    x_got(0, 3)
    for load in loads[4:]:
        load.wait()
    own0 = forward(0, 0)
    ring(1, 8)
    select(1, 1)
    far_y1 = y_send(1, 1)
    for p in (1, 2):
        y1[p].wait_recv()
        x_first(1, p)
    forward_sibling(0)
    y1[3].wait_recv()
    x_first(1, 3)
    for j in (0, 2, 1, 3):
        forward_tile(0, 0, *own0, j)
    x_got(1, 0)
    x_return_first(0, 0)
    x_return_first(0, 1)
    x_got(1, 1)
    x_got(1, 2)
    x_got(1, 3)
    far_y_got(1, far_y1)

    forward_sibling(1)
    own1 = forward(1, 0)
    forward_tile(1, 0, *own1, 0)
    forward_tile(1, 0, *own1, 2)
    x_return_first(1, 0)
    forward_tile(1, 0, *own1, 1)
    forward_tile(1, 0, *own1, 3)
    x_return_first(1, 1)
    x_return_second(0, 0)
    x_return_second(0, 1)
    x_return_second(1, 0)
    x_return_second(1, 1)
    y_return(0, 0)
    y_return(0, 1)
    some_grads(1)
    y_return(1, 0)
    y_return(1, 1)
    for g in range(2):
        unselect(0, g)
        z_odd(3, g)
        z_odd(1, g)
    some_grads(1)
    for g in range(2):
        unselect(1, g)
        z_even(8, g)
        z_odd(7, g)
        z_odd(5, g)
        some_grads(1)
    for k in (6, 4, 2):
        for g in range(2):
            z_even(k, g)
            some_grads(1)
    some_grads(len(tiles))
    for g in range(2):
        z_last(g)
    store(tg_ref, tg_hbm)
    for one in stores:
        one.wait()

    for made in started:
        made.wait_send()


def deliver(*refs):
    ins, outs, held, sems = refs[0:4], refs[4:8], refs[8:12], refs[12]
    fetch = [pltpu.make_async_copy(ins[i], held[i], sems.at[0, i]) for i in range(4)]
    store = [pltpu.make_async_copy(held[i], outs[i], sems.at[1, i]) for i in range(4)]
    for one in fetch:
        one.start()
    for i in range(4):
        fetch[i].wait()
        store[i].start()
    for one in store:
        one.wait()


def body(tokens, cotangent, expert_ids, gate_codes, w_gate, w_up, w_down):
    hbm = pl.BlockSpec(memory_space=pl.ANY)
    shapes = (
        jax.ShapeDtypeStruct((8, D), bf16),
        jax.ShapeDtypeStruct((1, H, D), bf16),
        jax.ShapeDtypeStruct((1, H, D), bf16),
        jax.ShapeDtypeStruct((1, H, D), bf16),
    )
    results = pl.pallas_call(
        kernel,
        out_shape=shapes,
        in_specs=[hbm] * 7,
        out_specs=(hbm,) * 4,
        scratch_shapes=[pltpu.VMEM((8, D), bf16)] * 2
        + [pltpu.VMEM((8, 8), jnp.int32)] * 2
        + [pltpu.VMEM((H, D), bf16)] * 3
        + [
            pltpu.VMEM((NZ, 16, D + META), bf16),
            pltpu.VMEM((NZ, 16, D + META), bf16),
            pltpu.VMEM((2, 2, 3, PIECE, 2 * D), bf16),
            pltpu.VMEM((2, 128, 128), bf16),
            pltpu.VMEM((1024, 2 * D), bf16),
            pltpu.VMEM((H, 1024), bf16),
            pltpu.VMEM((H, 1024), bf16),
            pltpu.VMEM((H, 1024), bf16),
            pltpu.VMEM((2, 256, D), bf16),
            pltpu.VMEM((2, 256, D), bf16),
            pltpu.VMEM((2, 256, D), bf16),
        ]
        + [pltpu.VMEM((2, PLANE, D), bf16)] * 6
        + [
            pltpu.VMEM((2, 2, 3, PIECE, HALF), bf16),
            pltpu.VMEM((2, 2, 4, PIECE, HALF), bf16),
            pltpu.VMEM((NZ, 16, HALF), f32),
            pltpu.VMEM((NZ, 16, HALF), bf16),
        ]
        + [pltpu.VMEM((4, 16, HALF), bf16)] * 4
        + [pltpu.VMEM((8, D), bf16)]
        + [pltpu.VMEM((H, D), bf16)] * 3
        + [
            pltpu.SemaphoreType.DMA((COPIES,)),
            pltpu.SemaphoreType.DMA((COPIES,)),
            pltpu.SemaphoreType.DMA((7,)),
            pltpu.SemaphoreType.DMA((4,)),
        ],
        compiler_params=pltpu.CompilerParams(
            collective_id=0, has_side_effects=True, vmem_limit_bytes=60 * 1024 * 1024
        ),
        name="expert_layer_backward",
    )(tokens, cotangent, expert_ids, gate_codes, w_gate, w_up, w_down)
    return pl.pallas_call(
        deliver,
        out_shape=shapes,
        in_specs=[hbm] * 4,
        out_specs=(hbm,) * 4,
        scratch_shapes=[pltpu.VMEM(shape.shape, bf16) for shape in shapes]
        + [pltpu.SemaphoreType.DMA((2, 4))],
        compiler_params=pltpu.CompilerParams(vmem_limit_bytes=60 * 1024 * 1024),
        name="deliver",
    )(*results)


def solution(mesh):
    placed = (
        P(("dp", "expert"), None),
        P(("dp", "expert"), None),
        P(("dp", "expert"), None),
        P(("dp", "expert"), None),
        P("expert", "dp", None),
        P("expert", "dp", None),
        P("expert", "dp", None),
    )
    return jax.shard_map(
        body,
        mesh=mesh,
        in_specs=placed,
        out_specs=(
            P(("dp", "expert"), None),
            P("expert", "dp", None),
            P("expert", "dp", None),
            P("expert", "dp", None),
        ),
        check_vma=False,
    )
```
